32 devices in a mesh: row: 4 (over x, core), col: 8 (over z, y).
Axes of the slice: x: 2, y: 2, z: 4, core: 2. Of those that a mesh axis runs over, the one named last changes fastest.
Arguments:
- density_tiles: float32 [3, 1024, 4096], P(None, ('row', 'col')), may hold values from -0.012 to 0.012
- tile_ids: int32 [1024], P(('row', 'col')), may hold values from 0 to 16383, as said below
- batch_blocks: int32 [32, 8], replicated, may hold values from 0 to 127, as said below
- basis_values: float32 [32, 512, 1024], P(('row', 'col')), may hold values from -6 to 6
- grid_weight: float32 [32, 1024], P(('row', 'col')), may hold values from 0.0002 to 0.002
- xc_kernel: float32 [32, 1024], P(('row', 'col')), may hold values from -2 to -0.5
- grid_coord: float32 [3, 32, 1024], P(None, ('row', 'col')), may hold values from -1 to 1
- orbitals: float32 [8192, 512], P('row'), may hold values from -1.5 to 1.5
- precond_diag: float32 [8192], P('row'), may hold values from 1 to 4
- orbital_energy: float32 [512], replicated, may hold values from -3 to -0.5
Outputs:
- new_density: float32 [3, 1024, 4096], P(None, ('row', 'col'))
The draws below stay inside these ranges and needn't reach their ends.
Inputs may be any that keep to these rules, and one draw needn't show every extreme that they name: `tile_ids`: the 32 slots of device (r, c), counted in row+col order, list distinct tiles I * 128 + J with I in the r-th range of 32 blocks and J in the c-th range of 16 blocks. `batch_blocks`: each row holds 8 ascending blocks, no two in the same range of 16 blocks, and exactly 2 of them in each range of 32 blocks.
All inputs are finite; a program needn't handle non-finite values.
Results may differ from the reference program's by a relative error of at most 0.0003.
Values sent between devices are 32-bit elements; how exact they have to be, the bound alone decides.
No kernel may reach another device: no remote copies, remote signals or barrier semaphores. Data moves between devices by JAX's collectives and lax.ppermute only.
A program may use at most 192 MiB of HBM per device.

```python
import math
import jax
import jax.numpy as jnp
from jax import lax

NB = 8192
TILE = 64
NOCC = 512
PTS = 1024
FB = 8
TPD = 32
NBLK = 128
ROWBLK = 32
COLBLK = 16
NBATCH = 32
TILES = 1024
N_ROW = 4
N_COL = 8


def draw_tile_ids(key, part):
    key_list = jax.random.split(jax.random.fold_in(key, 11), N_ROW * N_COL)

    def device_tiles(device_key, device):
        local_tiles = jax.random.permutation(device_key, ROWBLK * COLBLK)[:TPD]
        row_index = device // N_COL
        col_index = device % N_COL
        block_row = row_index * ROWBLK + local_tiles // COLBLK
        block_col = col_index * COLBLK + local_tiles % COLBLK
        return block_row * NBLK + block_col
    listed = jax.vmap(device_tiles)(key_list, jnp.arange(N_ROW * N_COL, dtype=jnp.int32))
    return listed.reshape(-1).astype(jnp.int32)


def draw_batch_blocks(key, part):
    per_range = FB // N_ROW
    range_count = N_COL // N_ROW
    key_list = jax.random.split(jax.random.fold_in(key, 23), NBATCH * N_ROW)

    def choose_blocks(range_key):
        first_key, second_key = jax.random.split(range_key)
        chosen = jnp.sort(jax.random.permutation(first_key, range_count)[:per_range])
        offsets = jax.random.randint(second_key, (per_range,), 0, COLBLK)
        return chosen * COLBLK + offsets
    local_blocks = jax.vmap(choose_blocks)(key_list).reshape(NBATCH, N_ROW, per_range)
    row_start = (jnp.arange(N_ROW, dtype=jnp.int32) * ROWBLK)[None, :, None]
    return (local_blocks + row_start).reshape(NBATCH, FB).astype(jnp.int32)


def levels(stream_key, shape, shards, smallest, largest):
    gain = 1.0
    for position, parts in shards:
        steps = jax.random.uniform(jax.random.fold_in(jax.random.fold_in(stream_key, 6), position), (parts,), jnp.float32, smallest / len(shards), largest / len(shards))
        gain = gain * jnp.repeat(jnp.exp(steps), shape[position] // parts).reshape((-1,) + (1,) * (len(shape) - 1 - position))
    return gain


def bell_draw(key, extent, spread, limit, pieces=(), kind=jnp.bfloat16):
    values = spread * jax.random.normal(key, extent, jnp.float32)
    if pieces:
        values = values * levels(key, extent, pieces, -0.22, 0.18)
    return jnp.clip(values, -limit, limit).astype(kind)


def setup_inputs(seed: int = 0) -> dict:
    splits = jax.random.split(jax.random.key(seed), 11)
    density_tiles = bell_draw(splits[0], (3, TILES, TILE * TILE), 0.002, 0.012, ((1, 32),), jnp.float32)
    tile_ids = draw_tile_ids(jax.random.fold_in(splits[10], 71), 0)
    batch_blocks = draw_batch_blocks(jax.random.fold_in(splits[10], 71), 0)
    basis_values = bell_draw(splits[3], (NBATCH, FB * TILE, PTS), 1.0, 6.0, ((0, 32),), jnp.float32)
    grid_weight = jnp.clip(jnp.exp(math.log(0.002) - 2.3025852 * jax.random.uniform(splits[4], (NBATCH, PTS), jnp.float32) ** levels(splits[4], (NBATCH, PTS), ((0, 32),), -0.2, 0.2)), 0.0002, 0.002)
    xc_kernel = jnp.clip(-2.0 + 1.5 * jax.random.uniform(splits[5], (NBATCH, PTS), jnp.float32) ** levels(splits[5], (NBATCH, PTS), ((0, 32),), -0.2, 0.2), -2.0, -0.5)
    grid_coord = jnp.clip(jax.random.uniform(splits[6], (3, NBATCH, PTS), jnp.float32, -1.0, 1.0) * levels(splits[6], (3, NBATCH, PTS), ((1, 32),), -0.4, 0.0), -1.0, 1.0)
    orbitals = bell_draw(splits[7], (NB, NOCC), 0.25, 1.5, ((0, 4),), jnp.float32)
    precond_diag = jnp.clip(1.0 + 3.0 * jax.random.uniform(splits[8], (NB,), jnp.float32) ** levels(splits[8], (NB,), ((0, 4),), -0.2, 0.2), 1.0, 4.0)
    orbital_energy = jnp.clip(jax.random.uniform(splits[9], (NOCC,), jnp.float32, -3.0, -0.5), -3.0, -0.5)
    return {"density_tiles": density_tiles, "tile_ids": tile_ids, "batch_blocks": batch_blocks, "basis_values": basis_values, "grid_weight": grid_weight, "xc_kernel": xc_kernel, "grid_coord": grid_coord, "orbitals": orbitals, "precond_diag": precond_diag, "orbital_energy": orbital_energy}


PRECISE = lax.Precision.HIGHEST


def reference(density_tiles, tile_ids, batch_blocks, basis_values, grid_weight, xc_kernel, grid_coord, orbitals, precond_diag, orbital_energy):
    block_count = NB // TILE
    tile_total = tile_ids.shape[0]
    tile_area = TILE * TILE
    batch_width = FB * TILE
    slot_table = jnp.full((block_count * block_count,), tile_total, dtype=jnp.int32)
    slot_table = slot_table.at[tile_ids].set(jnp.arange(tile_total, dtype=jnp.int32))
    padded = jnp.concatenate([density_tiles, jnp.zeros((3, 1, tile_area), dtype=jnp.float32)], axis=1)

    def one_batch(running, inputs):
        blocks, values, weight, kernel, coords = inputs
        wanted = (blocks[:, None] * block_count + blocks[None, :]).reshape(-1).astype(jnp.int32)
        slot_ids = jnp.take(slot_table, wanted, axis=0).astype(jnp.int32)
        tile_data = jnp.take(padded, slot_ids, axis=1).reshape(3, FB, FB, TILE, TILE)
        density = tile_data.transpose(0, 1, 3, 2, 4).reshape(3, batch_width, batch_width)
        projected = jnp.einsum("dmn,np->dmp", density, values, precision=PRECISE)
        response = jnp.sum(values[None] * projected, axis=1)
        potential = kernel[None] * response + coords
        weighted = values[None] * (weight[None] * potential)[:, None, :]
        hamiltonian = jnp.einsum("dmp,np->dmn", weighted, values, precision=PRECISE)
        ham_tiles = hamiltonian.reshape(3, FB, TILE, FB, TILE).transpose(0, 1, 3, 2, 4).reshape(3, FB * FB, tile_area)
        return running.at[:, slot_ids].add(ham_tiles), None

    inputs = (batch_blocks, basis_values, grid_weight, xc_kernel, jnp.moveaxis(grid_coord, 1, 0))
    accumulated, _ = lax.scan(one_batch, jnp.zeros((3, tile_total + 1, tile_area), dtype=jnp.float32), inputs)
    group_size = TPD
    group_count = tile_total // group_size
    ham_groups = accumulated[:, :tile_total].reshape(3, group_count, group_size, TILE, TILE).transpose(1, 0, 2, 3, 4)
    row_ids = (tile_ids // block_count).astype(jnp.int32).reshape(group_count, group_size)
    col_ids = (tile_ids % block_count).astype(jnp.int32).reshape(group_count, group_size)
    orbital_blocks = orbitals.reshape(block_count, TILE, NOCC)

    def add_group(running, inputs):
        ham_group, group_rows, group_cols = inputs
        picked = jnp.take(orbital_blocks, group_cols, axis=0)
        products = jnp.einsum("dsab,sbo->dsao", ham_group, picked, precision=PRECISE)
        return running.at[:, group_rows].add(products), None

    projected_orbitals, _ = lax.scan(add_group, jnp.zeros((3, block_count, TILE, NOCC), dtype=jnp.float32), (ham_groups, row_ids, col_ids))
    denominator = precond_diag.reshape(block_count, TILE)[None, :, :, None] - orbital_energy[None, None, None, :]
    response_orbs = -projected_orbitals / denominator

    def new_group(inputs):
        group_rows, group_cols = inputs
        x_rows = jnp.take(response_orbs, group_rows, axis=1)
        x_cols = jnp.take(response_orbs, group_cols, axis=1)
        c_rows = jnp.take(orbital_blocks, group_rows, axis=0)
        c_cols = jnp.take(orbital_blocks, group_cols, axis=0)
        renewed = jnp.einsum("dsao,sbo->dsab", x_rows, c_cols, precision=PRECISE)
        renewed = renewed + jnp.einsum("sao,dsbo->dsab", c_rows, x_cols, precision=PRECISE)
        return renewed.reshape(3, group_size, tile_area)

    renewed_all = lax.map(new_group, (row_ids, col_ids))
    return renewed_all.transpose(1, 0, 2, 3).reshape(3, tile_total, tile_area)
```

```python
import functools

import jax
import jax.numpy as jnp
from jax import lax
from jax.experimental import pallas as pl
from jax.experimental.pallas import tpu as pltpu
from jax.sharding import PartitionSpec as P

NB = 8192
TILE = 64
FB = 8
LANES = 2 * TILE
ROWS = TILE * TILE // LANES
F32 = jnp.float32
BF16 = jnp.bfloat16
NT = (((1,), (1,)), ((), ()))


def split(value):
    high = value.astype(BF16)
    return high, (value - high.astype(F32)).astype(BF16)


def dot(a, b):
    return jnp.dot(a, b, preferred_element_type=F32)


def dot_nt(a, b):
    return lax.dot_general(a, b, NT, preferred_element_type=F32)


def low_lanes(shape):
    return lax.broadcasted_iota(jnp.int32, shape, len(shape) - 1) < TILE


def params(mib):
    return pltpu.CompilerParams(vmem_limit_bytes=mib * 2**20)


VMEM = pl.BlockSpec(memory_space=pltpu.VMEM)
SMEM = pl.BlockSpec(memory_space=pltpu.SMEM)


def pick_kernel(slot_ref, tiles_ref, out_ref):
    count = out_ref.shape[0]

    def step(n, carry):
        slot = slot_ref[n]
        data = tiles_ref[:, jnp.maximum(slot, 0)]
        out_ref[n] = jnp.where(slot >= 0, data, 0.0)
        return carry

    lax.fori_loop(0, count, step, 0)


def pick_tiles(slots, tiles):
    nd = tiles.shape[0]
    return pl.pallas_call(
        pick_kernel,
        out_shape=jax.ShapeDtypeStruct((slots.shape[0], nd, ROWS, LANES), F32),
        in_specs=[SMEM, VMEM],
        out_specs=VMEM,
        compiler_params=params(32),
        name="pick_tiles",
    )(slots, tiles)


def batch_kernel(
    per_range, col_count, col_ref, tiles_ref, basis_ref, weight_ref, xc_ref, coord_ref, out_ref,
    bh, bl, wh, wl, square,
):
    nd = tiles_ref.shape[1]
    width, pts = basis_ref.shape
    low = low_lanes((ROWS, LANES))
    if col_count > FB:
        out_ref[...] = jnp.zeros(out_ref.shape, F32)

    def place(i, j):
        owner = (i // per_range) * col_count + col_ref[j]
        return owner * per_range + i % per_range

    high, rest = split(basis_ref[...])
    bh[...] = high
    bl[...] = rest

    def direction(d, carry):
        for i in range(FB):
            for jj in range(FB // 2):
                first = tiles_ref[place(i, 2 * jj), d]
                second = tiles_ref[place(i, 2 * jj + 1), d]
                square[jj, pl.ds(i * TILE, ROWS, stride=2), :] = jnp.where(
                    low, first, pltpu.roll(second, TILE, 1)
                )
                square[jj, pl.ds(i * TILE + 1, ROWS, stride=2), :] = jnp.where(
                    low, pltpu.roll(first, TILE, 1), second
                )
        eh, el = split(jnp.concatenate([square[jj] for jj in range(FB // 2)], axis=1))
        piece = 256
        for start in range(0, pts, piece):
            cols = slice(start, start + piece)
            projected = dot(eh, bh[:, cols]) + dot(eh, bl[:, cols]) + dot(el, bh[:, cols])
            values = basis_ref[:, cols]
            response = jnp.sum(values * projected, axis=0, keepdims=True)
            potential = xc_ref[:, cols] * response + coord_ref[d, :, cols]
            weighted = values * (weight_ref[:, cols] * potential)
            high, rest = split(weighted)
            wh[:, cols] = high
            wl[:, cols] = rest
        for start in range(0, width, piece):
            rows = slice(start, start + piece)
            value = (
                dot_nt(wh[...], bh[rows]) + dot_nt(wh[...], bl[rows]) + dot_nt(wl[...], bh[rows])
            )
            for lane in range(0, piece, LANES):
                square[(start + lane) // LANES] = value[:, lane : lane + LANES]
        for i in range(FB):
            for jj in range(FB // 2):
                even = square[jj, pl.ds(i * TILE, ROWS, stride=2), :]
                odd = square[jj, pl.ds(i * TILE + 1, ROWS, stride=2), :]
                out_ref[place(i, 2 * jj), d] = jnp.where(low, even, pltpu.roll(odd, TILE, 1))
                out_ref[place(i, 2 * jj + 1), d] = jnp.where(low, pltpu.roll(even, TILE, 1), odd)
        return carry

    lax.fori_loop(0, nd, direction, 0)


def batch_tiles(per_range, col_count, cols, tiles, basis, weight, xc, coord):
    width, pts = basis.shape
    return pl.pallas_call(
        functools.partial(batch_kernel, per_range, col_count),
        out_shape=jax.ShapeDtypeStruct(tiles.shape, F32),
        in_specs=[SMEM] + [VMEM] * 5,
        out_specs=VMEM,
        scratch_shapes=[
            pltpu.VMEM((width, pts), BF16),
            pltpu.VMEM((width, pts), BF16),
            pltpu.VMEM((width, pts), BF16),
            pltpu.VMEM((width, pts), BF16),
            pltpu.VMEM((width // LANES, width, LANES), F32),
        ],
        compiler_params=params(48),
        name="batch_tiles",
    )(cols, tiles, basis, weight, xc, coord)


def add_kernel(slot_ref, tiles_ref, out_ref):
    count = tiles_ref.shape[0]
    out_ref[...] = jnp.zeros(out_ref.shape, F32)

    def step(n, carry):
        slot = slot_ref[n]

        @pl.when(slot >= 0)
        def _():
            out_ref[slot] += tiles_ref[n]

        return carry

    lax.fori_loop(0, count, step, 0)


def add_tiles(slots, tiles, slot_count):
    return pl.pallas_call(
        add_kernel,
        out_shape=jax.ShapeDtypeStruct((slot_count,) + tiles.shape[1:], F32),
        in_specs=[SMEM, VMEM],
        out_specs=VMEM,
        compiler_params=params(32),
        name="add_tiles",
    )(slots, tiles)


def rows_kernel(chunk_count, fresh, *refs):
    refs = list(refs)
    col_ref, row_id, col_id = refs[:3]
    chunks = refs[3 : 3 + chunk_count]
    orbs = refs[3 + chunk_count : 3 + 2 * chunk_count]
    rest = refs[3 + 2 * chunk_count :]
    if fresh:
        out_ref, stacked = rest
        out_ref[...] = jnp.zeros(out_ref.shape, F32)
    else:
        in_ref, out_ref, stacked = rest
        out_ref[...] = in_ref[...]
    accumulate(chunks, orbs, row_id, col_id, out_ref, stacked)


def accumulate(chunks, orbs, row_id, col_id, out_ref, stacked):
    low = low_lanes((ROWS, LANES))
    offset = 0
    for chunk, orb in zip(chunks, orbs):
        count, nd = chunk.shape[:2]

        def stack(b, carry, orb=orb):
            high, rest = split(orb[pl.ds(pl.multiple_of(b * TILE, TILE), TILE), :])
            stacked[b, 0 * TILE : 1 * TILE] = high
            stacked[b, 1 * TILE : 2 * TILE] = rest
            stacked[b, 2 * TILE : 3 * TILE] = high
            stacked[b, 3 * TILE : 4 * TILE] = rest
            return carry

        lax.fori_loop(0, orb.shape[0] // TILE, stack, 0)

        def step(s, carry, chunk=chunk, offset=offset, nd=nd):
            parts = []
            for d in range(nd):
                tile = chunk[s, d]
                turned = pltpu.roll(tile, TILE, 1)
                for value in (jnp.where(low, tile, turned), jnp.where(low, turned, tile)):
                    parts.append(jnp.concatenate(split(value), axis=1))
            left = jnp.concatenate(parts, axis=0)
            product = dot(left, stacked[col_id[offset + s]])
            out_ref[row_id[offset + s]] += product
            return carry

        lax.fori_loop(0, count, step, 0)
        offset += count


def add_rows(total, chunks, places, row_ids, col_ids, orbitals, row_blocks, col_width):
    nd = chunks[0].shape[1]
    count = len(chunks)
    nocc = orbitals.shape[1]
    shape = jax.ShapeDtypeStruct((row_blocks, nd * TILE, nocc), F32)
    whole = lambda a: pl.BlockSpec(a.shape, lambda g, *_, n=len(a.shape): (0,) * n)
    in_specs = [whole(c) for c in chunks]
    for k in range(count):
        in_specs.append(pl.BlockSpec((col_width, nocc), lambda g, p, r, c, k=k: (p[k], 0)))
    args = list(chunks) + [orbitals] * count
    aliases = {}
    if total is not None:
        in_specs.append(whole(shape))
        args.append(total)
        aliases = {3 + len(args) - 1: 0}
    return pl.pallas_call(
        functools.partial(rows_kernel, count, total is None),
        out_shape=shape,
        grid_spec=pltpu.PrefetchScalarGridSpec(
            num_scalar_prefetch=3,
            grid=(1,),
            in_specs=in_specs,
            out_specs=whole(shape),
            scratch_shapes=[pltpu.VMEM((col_width // TILE, 4 * TILE, nocc), BF16)],
        ),
        input_output_aliases=aliases,
        compiler_params=params(60),
        name="add_rows",
    )(places, row_ids, col_ids, *args)


def response_kernel(
    nd, piece_blocks, part_ref, total_ref, diag_ref, energy_ref, out_ref, piece_ref, square
):
    blocks = total_ref.shape[0]
    first = part_ref[0] * piece_blocks

    def step(b, carry):
        inverse = -1.0 / (diag_ref[b] - energy_ref[...])
        inside = jnp.logical_and(b >= first, b < first + piece_blocks)
        for d in range(nd):
            rows = slice(d * TILE, (d + 1) * TILE)
            out_ref[b, rows] = total_ref[b, rows] * inverse

        @pl.when(inside)
        def _():
            for d in range(nd):
                for k in range(square.shape[0]):
                    lanes = slice(k * LANES, (k + 1) * LANES)
                    for parity in range(2):
                        start = d * TILE + parity * ROWS
                        square[k, pl.ds(parity, ROWS, stride=2), :] = out_ref[
                            b, start : start + ROWS, lanes
                        ]
                    piece_ref[d, b - first, :, lanes] = square[k]

        return carry

    lax.fori_loop(0, blocks, step, 0)


def response(total, diag, energy, part, piece_blocks):
    blocks, rows, nocc = total.shape
    nd = rows // TILE
    return pl.pallas_call(
        functools.partial(response_kernel, nd, piece_blocks),
        out_shape=(
            jax.ShapeDtypeStruct(total.shape, F32),
            jax.ShapeDtypeStruct((nd, piece_blocks, TILE, nocc), F32),
        ),
        in_specs=[SMEM] + [VMEM] * 3,
        out_specs=(VMEM, VMEM),
        scratch_shapes=[pltpu.VMEM((nocc // LANES, TILE, LANES), F32)],
        compiler_params=params(60),
        name="response_orbitals",
    )(part, total, diag, energy)


def first_kernel(nd, row_id, col_id, x_ref, orb_ref, out_ref, both):
    low = low_lanes((ROWS, LANES))

    def stack(b, carry):
        high, rest = split(orb_ref[pl.ds(pl.multiple_of(b * TILE, TILE), TILE), :])
        both[b, 0:TILE] = high
        both[b, TILE : 2 * TILE] = rest
        return carry

    lax.fori_loop(0, both.shape[0], stack, 0)

    def step(s, carry):
        high, rest = split(x_ref[row_id[s]])
        pair = both[col_id[s]]
        value = dot_nt(high, pair) + dot_nt(rest, pair)
        value = value + pltpu.roll(value, TILE, 1)
        for d in range(nd):
            start = d * TILE
            even = value[start : start + ROWS]
            odd = value[start + ROWS : start + TILE]
            out_ref[d, s] = jnp.where(low, even, odd)
        return carry

    lax.fori_loop(0, out_ref.shape[1], step, 0)


def first_term(row_ids, col_ids, x, orb_cols):
    slots = row_ids.shape[0]
    nd = x.shape[1] // TILE
    nocc = x.shape[2]
    return pl.pallas_call(
        functools.partial(first_kernel, nd),
        out_shape=jax.ShapeDtypeStruct((nd, slots, ROWS, LANES), F32),
        in_specs=[SMEM, SMEM, VMEM, VMEM],
        out_specs=VMEM,
        scratch_shapes=[
            pltpu.VMEM((orb_cols.shape[0] // TILE, 2 * TILE, nocc), BF16),
        ],
        compiler_params=params(60),
        name="first_term",
    )(row_ids, col_ids, x, orb_cols)


def second_kernel(nd, row_id, col_id, x_ref, orb_ref, first_ref, out_ref, square):
    low = low_lanes((ROWS, LANES))

    def step(s, carry):
        block = pl.ds(pl.multiple_of(row_id[s] * TILE, TILE), TILE)
        high, rest = split(orb_ref[block, :])
        left = jnp.concatenate([high, rest], axis=0)
        for d in range(nd):
            x_high, x_rest = split(x_ref[d, col_id[s]])
            pair = jnp.concatenate([x_high, x_rest], axis=0)
            value = dot_nt(left, pair)
            value = value[:TILE] + value[TILE:]
            square[...] = value + pltpu.roll(value, TILE, 1)
            even = square[pl.ds(0, ROWS, stride=2), :]
            odd = square[pl.ds(1, ROWS, stride=2), :]
            out_ref[d, s] = first_ref[d, s] + jnp.where(low, even, odd)
        return carry

    lax.fori_loop(0, out_ref.shape[1], step, 0)


def second_term(row_ids, col_ids, x_cols, orbitals, first):
    nd = x_cols.shape[0]
    return pl.pallas_call(
        functools.partial(second_kernel, nd),
        out_shape=jax.ShapeDtypeStruct(first.shape, F32),
        in_specs=[SMEM, SMEM, VMEM, VMEM, VMEM],
        out_specs=VMEM,
        scratch_shapes=[pltpu.VMEM((TILE, LANES), F32)],
        compiler_params=params(60),
        name="second_term",
    )(row_ids, col_ids, x_cols, orbitals, first)


def ring_order(count):
    return list(range(0, count, 2)) + list(range(count - 1, 0, -2))


def row_broadcast(value, row_count, col_count, ratio, own_row, own_col):
    away = own_row ^ (own_col // ratio)
    bit = row_count // 2
    passed = 0
    while bit:
        pairs = []
        for c in range(col_count):
            for r in range(row_count):
                if (r ^ (c // ratio)) & ~passed == 0:
                    pairs.append((r * col_count + c, (r ^ bit) * col_count + c))
        got = lax.ppermute(value, ("row", "col"), pairs)
        passed |= bit
        taken = jnp.logical_and((away & bit) != 0, (away & ~passed) == 0)
        value = jnp.where(taken, got, value)
        bit //= 2
    return value


def local(
    density_tiles,
    tile_ids,
    batch_blocks,
    basis_values,
    grid_weight,
    xc_kernel,
    grid_coord,
    orbitals,
    precond_diag,
    orbital_energy,
):
    row_count = lax.axis_size("row")
    col_count = lax.axis_size("col")
    device_count = row_count * col_count
    own_row = lax.axis_index("row")
    own_col = lax.axis_index("col")
    own_index = own_row * col_count + own_col
    block_count = NB // TILE
    row_blocks = block_count // row_count
    col_blocks = block_count // col_count
    per_range = FB // row_count
    slot_count = tile_ids.shape[0]
    ratio = col_count // row_count
    col_width = col_blocks * TILE
    nd = density_tiles.shape[0]
    nocc = orbitals.shape[1]

    ask = batch_blocks
    match = ask // col_blocks == own_col
    ask_col = jnp.sum(jnp.where(match, ask, 0), axis=1)
    ask_row = lax.dynamic_slice_in_dim(ask, own_row * per_range, per_range, 1)
    wanted = jnp.where(jnp.any(match, axis=1)[:, None], ask_row * block_count + ask_col[:, None], -1)
    hit = wanted.reshape(-1)[:, None] == tile_ids[None, :]
    slots = jnp.max(jnp.where(hit, jnp.arange(slot_count, dtype=jnp.int32)[None, :], -1), axis=1)
    own_cols = lax.dynamic_slice_in_dim(ask, own_index, 1, 0)[0] // col_blocks

    listed = lax.all_gather(tile_ids, "col", axis=0, tiled=False)
    listed_rows = listed // block_count - own_row * row_blocks
    listed_cols = listed % col_blocks
    local_rows = tile_ids // block_count - own_row * row_blocks
    local_cols = tile_ids % col_blocks
    all_orbitals = lax.all_gather(orbitals, "row", axis=0, tiled=True)

    tiles = density_tiles.reshape(nd, slot_count, ROWS, LANES)
    picked = pick_tiles(slots, tiles)
    exchange = lambda a: lax.all_to_all(
        a.reshape(device_count, -1, LANES), ("row", "col"), split_axis=0, concat_axis=0, tiled=True
    ).reshape(a.shape)
    arrived = exchange(picked)
    built = batch_tiles(
        per_range, col_count, own_cols, arrived, basis_values[0], grid_weight, xc_kernel, grid_coord
    )
    returned = exchange(built)
    ham = add_tiles(slots, returned, slot_count)

    order = ring_order(col_count)
    place = [order.index(c) for c in range(col_count)]
    forward = [(order[i], order[(i + 1) % col_count]) for i in range(col_count)]
    backward = [(b, a) for a, b in forward]
    ring = jnp.asarray(order, jnp.int32)
    at = jnp.asarray(place, jnp.int32)[own_col]

    def rows(total, chunks, offsets, starts):
        cols = [ring[(at + o) % col_count] for o in offsets]
        take = lambda table: jnp.concatenate(
            [table[c, s : s + k.shape[0]] for c, s, k in zip(cols, starts, chunks)]
        )
        return add_rows(
            total, chunks, jnp.stack(cols), take(listed_rows), take(listed_cols), all_orbitals,
            row_blocks, col_width,
        )

    up = down = ham
    half = slot_count // 2
    total = None
    held = [(ham,)]
    offsets = [(0,)]
    for step in range(1, col_count // 2):
        up = lax.ppermute(up, "col", forward)
        down = lax.ppermute(down, "col", backward)
        held.append((up, down))
        offsets.append((-step, step))
    up = lax.ppermute(up[:half], "col", forward)
    down = lax.ppermute(down[half:], "col", backward)
    held.append((up, down))
    offsets.append((col_count // 2, col_count // 2))
    for chunks, offs in zip(held, offsets):
        starts = [0, half] if chunks[0].shape[0] == half else [0] * len(chunks)
        total = rows(total, chunks, offs, starts)

    diag = precond_diag.reshape(row_blocks, ROWS, 2).swapaxes(1, 2).reshape(row_blocks, TILE, 1)
    part = (own_col % ratio).reshape(1)
    x, piece = response(total, diag, orbital_energy[None], part, col_blocks)
    x_cols = row_broadcast(piece, row_count, col_count, ratio, own_row, own_col)
    orb_cols = lax.dynamic_slice_in_dim(all_orbitals, own_col * col_width, col_width, 0)
    first = first_term(local_rows, local_cols, x, orb_cols)
    renewed = second_term(local_rows, local_cols, x_cols, orbitals, first)
    return renewed.reshape(nd, slot_count, TILE * TILE)


def solution(mesh):
    placed = (
        P(None, ("row", "col"), None),
        P(("row", "col")),
        P(),
        P(("row", "col"), None, None),
        P(("row", "col"), None),
        P(("row", "col"), None),
        P(None, ("row", "col"), None),
        P("row", None),
        P("row"),
        P(),
    )
    return jax.shard_map(
        local, mesh=mesh, in_specs=placed, out_specs=P(None, ("row", "col"), None), check_vma=False
    )
```

```python
import functools

import jax
import jax.numpy as jnp
from jax import lax
from jax.experimental import pallas as pl
from jax.experimental.pallas import tpu as pltpu
from jax.sharding import PartitionSpec as P

NB = 8192
TILE = 64
FB = 8
LANES = 2 * TILE
ROWS = TILE * TILE // LANES
F32 = jnp.float32
BF16 = jnp.bfloat16
NT = (((1,), (1,)), ((), ()))


def split(value):
    high = value.astype(BF16)
    return high, (value - high.astype(F32)).astype(BF16)


def dot(a, b):
    return jnp.dot(a, b, preferred_element_type=F32)


def dot_nt(a, b):
    return lax.dot_general(a, b, NT, preferred_element_type=F32)


def low_lanes(shape):
    return lax.broadcasted_iota(jnp.int32, shape, len(shape) - 1) < TILE


def params(mib):
    return pltpu.CompilerParams(vmem_limit_bytes=mib * 2**20)


VMEM = pl.BlockSpec(memory_space=pltpu.VMEM)
SMEM = pl.BlockSpec(memory_space=pltpu.SMEM)


def in_groups(count, body, group=16):
    if count % group:
        group = 1

    def step(g, carry):
        body([g * group + u for u in range(group)])
        return carry

    lax.fori_loop(0, count // group, step, 0)


def pick_kernel(slot_ref, tiles_ref, ids_ref, out_ref, rows):
    nd, slots, area = tiles_ref.shape
    per_range = slot_ref.shape[0] // out_ref.shape[0]
    for d in range(nd):
        for start in range(0, slots, 8):
            for k in range(area // LANES):
                rows[d, pl.ds(start * ROWS + k, 8, stride=ROWS), :] = tiles_ref[
                    d, start : start + 8, k * LANES : (k + 1) * LANES
                ]

    def device(index):
        for n in index:
            for k in range(per_range):
                slot = slot_ref[n * per_range + k]
                first = pl.multiple_of(jnp.maximum(slot, 0) * ROWS, ROWS)
                for d in range(nd):
                    out_ref[n, (k * nd + d) * ROWS : (k * nd + d + 1) * ROWS] = jnp.where(
                        slot >= 0, rows[d, pl.ds(first, ROWS), :], 0.0
                    )
            out_ref[n, per_range * nd * ROWS :] = ids_ref[...]

    in_groups(out_ref.shape[0], device, 2)


def pick_tiles(slots, tiles, ids, device_count):
    nd, count, area = tiles.shape
    rows = slots.shape[0] // device_count * nd * ROWS + ids.shape[0]
    return pl.pallas_call(
        pick_kernel,
        out_shape=jax.ShapeDtypeStruct((device_count, rows, LANES), F32),
        in_specs=[SMEM, VMEM, VMEM],
        out_specs=VMEM,
        scratch_shapes=[pltpu.VMEM((nd, count * ROWS, LANES), F32)],
        compiler_params=params(32),
        name="pick_tiles",
    )(slots, tiles, ids)


def batch_kernel(
    per_range, col_count, col_ref, tiles_ref, basis_ref, weight_ref, xc_ref, coord_ref, out_ref,
    bh, bl, wh, wl, square,
):
    nd = coord_ref.shape[0]
    width, pts = basis_ref.shape
    low = low_lanes((ROWS, LANES))
    if col_count > FB:
        out_ref[...] = jnp.zeros(out_ref.shape, F32)

    def place(i, j, d):
        owner = (i // per_range) * col_count + col_ref[j]
        return owner, pl.ds(pl.multiple_of((i % per_range * nd + d) * ROWS, ROWS), ROWS)

    high, rest = split(basis_ref[...])
    bh[...] = high
    bl[...] = rest

    def direction(d, carry):
        for i in range(FB):
            for jj in range(FB // 2):
                first = tiles_ref[place(i, 2 * jj, d)]
                second = tiles_ref[place(i, 2 * jj + 1, d)]
                square[jj, pl.ds(i * TILE, ROWS, stride=2), :] = jnp.where(
                    low, first, pltpu.roll(second, TILE, 1)
                )
                square[jj, pl.ds(i * TILE + 1, ROWS, stride=2), :] = jnp.where(
                    low, pltpu.roll(first, TILE, 1), second
                )
        eh, el = split(jnp.concatenate([square[jj] for jj in range(FB // 2)], axis=1))
        piece = 256
        for start in range(0, pts, piece):
            cols = slice(start, start + piece)
            projected = dot(eh, bh[:, cols]) + dot(eh, bl[:, cols]) + dot(el, bh[:, cols])
            values = basis_ref[:, cols]
            response = jnp.sum(values * projected, axis=0, keepdims=True)
            potential = xc_ref[:, cols] * response + coord_ref[d, :, cols]
            weighted = values * (weight_ref[:, cols] * potential)
            high, rest = split(weighted)
            wh[:, cols] = high
            wl[:, cols] = rest
        for start in range(0, width, piece):
            rows = slice(start, start + piece)
            value = (
                dot_nt(wh[...], bh[rows]) + dot_nt(wh[...], bl[rows]) + dot_nt(wl[...], bh[rows])
            )
            for lane in range(0, piece, LANES):
                square[(start + lane) // LANES] = value[:, lane : lane + LANES]
        for i in range(FB):
            for jj in range(FB // 2):
                even = square[jj, pl.ds(i * TILE, ROWS, stride=2), :]
                odd = square[jj, pl.ds(i * TILE + 1, ROWS, stride=2), :]
                out_ref[place(i, 2 * jj, d)] = jnp.where(low, even, pltpu.roll(odd, TILE, 1))
                out_ref[place(i, 2 * jj + 1, d)] = jnp.where(low, pltpu.roll(even, TILE, 1), odd)
        return carry

    lax.fori_loop(0, nd, direction, 0)


def batch_tiles(per_range, col_count, cols, tiles, basis, weight, xc, coord):
    width, pts = basis.shape
    return pl.pallas_call(
        functools.partial(batch_kernel, per_range, col_count),
        out_shape=jax.ShapeDtypeStruct(
            (tiles.shape[0], per_range * coord.shape[0] * ROWS, LANES), F32
        ),
        in_specs=[SMEM] + [VMEM] * 5,
        out_specs=VMEM,
        scratch_shapes=[
            pltpu.VMEM((width, pts), BF16),
            pltpu.VMEM((width, pts), BF16),
            pltpu.VMEM((width, pts), BF16),
            pltpu.VMEM((width, pts), BF16),
            pltpu.VMEM((width // LANES, width, LANES), F32),
        ],
        compiler_params=params(48),
        name="batch_tiles",
    )(cols, tiles, basis, weight, xc, coord)


def add_kernel(slot_ref, tiles_ref, *out_refs):
    for out_ref in out_refs:
        out_ref[...] = jnp.zeros(out_ref.shape, F32)

    nd = len(out_refs)
    per_range = slot_ref.shape[0] // tiles_ref.shape[0]

    def step(n, carry):
        for k in range(per_range):
            slot = slot_ref[n * per_range + k]

            @pl.when(slot >= 0)
            def _(slot=slot, k=k):
                for d, out_ref in enumerate(out_refs):
                    start = (k * nd + d) * ROWS
                    out_ref[slot] += tiles_ref[n, start : start + ROWS]

        return carry

    lax.fori_loop(0, tiles_ref.shape[0], step, 0)


def add_tiles(slots, tiles, slot_count, nd):
    return pl.pallas_call(
        add_kernel,
        out_shape=[jax.ShapeDtypeStruct((slot_count, ROWS, LANES), F32)] * nd,
        in_specs=[SMEM, VMEM],
        out_specs=[VMEM] * nd,
        compiler_params=params(32),
        name="add_tiles",
    )(slots, tiles)


def split_kernel(orb_ref, out_ref):
    def blocks(index):
        for b in index:
            high, rest = split(orb_ref[pl.ds(pl.multiple_of(b * TILE, TILE), TILE), :])
            out_ref[b, :TILE] = high
            out_ref[b, TILE:] = rest

    in_groups(out_ref.shape[0], blocks, 2)


def split_orbitals(orbitals, parts):
    count, nocc = orbitals.shape
    return pl.pallas_call(
        split_kernel,
        out_shape=jax.ShapeDtypeStruct((count // TILE, 2 * TILE, nocc), BF16),
        grid=(parts,),
        in_specs=[pl.BlockSpec((count // parts, nocc), lambda g: (g, 0))],
        out_specs=pl.BlockSpec((count // parts // TILE, 2 * TILE, nocc), lambda g: (g, 0, 0)),
        compiler_params=params(32),
        cost_estimate=pl.CostEstimate(
            flops=0, bytes_accessed=8 * count * nocc, transcendentals=0
        ),
        name="split_orbitals",
    )(orbitals)


def accumulate(chunks, orbs, row_id, col_id, sums):
    low = low_lanes((ROWS, LANES))
    nd = len(sums)
    offset = 0
    for chunk, orb in zip(chunks, orbs):

        def tiles(index, chunk=chunk, orb=orb, offset=offset):
            products = []
            for s in index:
                left = []
                for d in range(nd):
                    tile = chunk[d][s]
                    turned = pltpu.roll(tile, TILE, 1)
                    for value in (jnp.where(low, tile, turned), jnp.where(low, turned, tile)):
                        left.append(jnp.concatenate(split(value), axis=1))
                left = jnp.concatenate(left, axis=0)
                pair = orb[col_id[offset + s]]
                products.append(dot(left, jnp.concatenate([pair, pair], axis=0)))
            for s, product in zip(index, products):
                block = row_id[offset + s]
                for d in range(nd):
                    sums[d][block] += product[d * TILE : (d + 1) * TILE]

        in_groups(chunk[0].shape[0], tiles)
        offset += chunk[0].shape[0]


def whole(a):
    return pl.BlockSpec(a.shape, lambda g, *_, n=len(a.shape): (0,) * n)


def orb_spec(blocks, orbs, which):
    return pl.BlockSpec((blocks,) + orbs.shape[1:], lambda g, *t: (which(*t), 0, 0))


def call(kernel, name, tables, args, specs, out, scratch, products, mib=60):
    single = not isinstance(out, (tuple, list))
    return pl.pallas_call(
        kernel,
        out_shape=out,
        grid_spec=pltpu.PrefetchScalarGridSpec(
            num_scalar_prefetch=len(tables),
            grid=(1,),
            in_specs=specs,
            out_specs=whole(out) if single else [whole(o) for o in out],
            scratch_shapes=scratch,
        ),
        compiler_params=params(mib),
        cost_estimate=pl.CostEstimate(
            flops=products * 100_000_000, bytes_accessed=2**23, transcendentals=0
        ),
        name=name,
    )(*tables, *args)


def rows_kernel(count, nd, row_id, col_id, place_ref, *refs):
    chunks = [refs[nd * k : nd * (k + 1)] for k in range(count)]
    orbs, sums = refs[nd * count : (nd + 1) * count], refs[(nd + 1) * count :]
    for total in sums:
        total[...] = jnp.zeros(total.shape, F32)
    accumulate(chunks, orbs, row_id, col_id, sums)


def add_rows(chunks, where, orbs, row_blocks, col_blocks):
    count = len(chunks)
    nd = len(chunks[0])
    flat = [c for chunk in chunks for c in chunk]
    specs = [whole(c) for c in flat]
    specs += [orb_spec(col_blocks, orbs, lambda r, c, p, k=k: p[k]) for k in range(count)]
    out = jax.ShapeDtypeStruct((row_blocks, TILE, orbs.shape[2]), F32)
    return call(
        functools.partial(rows_kernel, count, nd), "add_rows", where, flat + [orbs] * count, specs,
        [out] * nd, [], count * flat[0].shape[0],
    )


def piece_kernel(count, row_id, col_id, place_ref, *refs):
    chunks, orbs, refs = refs[:count], refs[count : 2 * count - 1], refs[2 * count - 1 :]
    in_ref, diag_ref, energy_ref, piece_ref, total_ref, sums, square, sem = refs
    load = pltpu.make_async_copy(in_ref, sums, sem)
    load.start()
    load.wait()
    accumulate([[c] for c in chunks], orbs + orbs[-1:], row_id, col_id, [sums])
    store = pltpu.make_async_copy(sums, total_ref, sem)
    store.start()
    first = place_ref[count - 1] * piece_ref.shape[0]

    def blocks(index):
        for b in index:
            value = sums[first + b] * (-1.0 / (diag_ref[first + b] - energy_ref[...]))
            for k in range(square.shape[1]):
                lanes = slice(k * LANES, (k + 1) * LANES)
                for parity in range(2):
                    square[b % 2, k, pl.ds(parity, ROWS, stride=2), :] = value[
                        parity * ROWS : (parity + 1) * ROWS, lanes
                    ]
                piece_ref[b, :, lanes] = square[b % 2, k]

    in_groups(piece_ref.shape[0], blocks, 2)
    store.wait()


def response_piece(total, chunks, where, orbs, diag, energy, col_blocks):
    count = len(chunks)
    nocc = orbs.shape[2]
    hbm = pl.BlockSpec(memory_space=pl.ANY)
    specs = [whole(c) for c in chunks]
    specs += [orb_spec(col_blocks, orbs, lambda r, c, p, k=k: p[k]) for k in range(count - 1)]
    specs += [hbm, whole(diag), whole(energy)]
    piece = jax.ShapeDtypeStruct((col_blocks, TILE, nocc), F32)
    return pl.pallas_call(
        functools.partial(piece_kernel, count),
        out_shape=(piece, jax.ShapeDtypeStruct(total.shape, F32)),
        grid_spec=pltpu.PrefetchScalarGridSpec(
            num_scalar_prefetch=3,
            grid=(1,),
            in_specs=specs,
            out_specs=(whole(piece), hbm),
            scratch_shapes=[
                pltpu.VMEM(total.shape, F32),
                pltpu.VMEM((2, nocc // LANES, TILE, LANES), F32),
                pltpu.SemaphoreType.DMA,
            ],
        ),
        compiler_params=params(60),
        cost_estimate=pl.CostEstimate(
            flops=20_000_000_000, bytes_accessed=2**23, transcendentals=0
        ),
        name="response_piece",
    )(*where, *chunks, *[orbs] * (count - 1), total, diag, energy)


def first_kernel(nd, row_id, col_id, place_ref, *refs):
    totals, (diag_ref, energy_ref, orb_ref, out_ref) = refs[:nd], refs[nd:]
    low = low_lanes((ROWS, LANES))

    def tiles(index):
        for s in index:
            block = row_id[s]
            inverse = -1.0 / (diag_ref[block] - energy_ref[...])
            left = [part for total in totals for part in split(total[block] * inverse)]
            value = dot_nt(jnp.concatenate(left, axis=0), orb_ref[col_id[s]])
            for d in range(nd):
                start = 2 * d * TILE
                tile = value[start : start + TILE] + value[start + TILE : start + 2 * TILE]
                tile = tile + pltpu.roll(tile, TILE, 1)
                out_ref[d, s] = jnp.where(low, tile[:ROWS], tile[ROWS:])

    in_groups(out_ref.shape[1], tiles, 8)


def first_term(own, places, totals, diag, energy, orbs, col_blocks):
    nd, slots = len(totals), own[0].shape[0]
    specs = [whole(a) for a in [*totals, diag, energy]]
    specs.append(orb_spec(col_blocks, orbs, lambda r, c, p: p[2]))
    return call(
        functools.partial(first_kernel, nd), "first_term", [*own, places],
        [*totals, diag, energy, orbs], specs,
        jax.ShapeDtypeStruct((nd, slots, ROWS, LANES), F32), [], slots,
    )


def second_kernel(directions, way_count, last, row_id, col_id, place_ref, *refs):
    count = len(directions)
    ways = [refs[d * way_count : (d + 1) * way_count] for d in range(count)]
    refs = refs[count * way_count :]
    orb_ref, first_ref, refs = refs[0], refs[1], refs[2:]
    if last:
        done_ref, refs = refs[0], refs[1:]
    out_ref, x_ref, square, sem = refs[:4]
    for d in range(count):
        for k, way in enumerate(ways[d]):

            @pl.when(place_ref[1] == k)
            def _(way=way, d=d):
                pltpu.make_async_copy(way, x_ref.at[d], sem.at[d]).start()

    for d in range(count):
        pltpu.make_async_copy(ways[d][0], x_ref.at[d], sem.at[d]).wait()
    low = low_lanes((ROWS, LANES))
    slots = first_ref.shape[1]

    def tiles(index):
        for u, s in enumerate(index):
            right = [part for d in range(count) for part in split(x_ref[d, col_id[s]])]
            value = dot_nt(orb_ref[row_id[s]], jnp.concatenate(right, axis=0))
            value = value[:TILE] + value[TILE:]
            for d in range(count):
                tile = value[:, d * LANES : (d + 1) * LANES]
                square[d, u] = tile + pltpu.roll(tile, TILE, 1)
        for u, s in enumerate(index):
            for d in range(count):
                even = square[d, u, pl.ds(0, ROWS, stride=2), :]
                odd = square[d, u, pl.ds(1, ROWS, stride=2), :]
                value = first_ref[directions[d], s] + jnp.where(low, even, odd)
                if last:
                    refs[4][d, pl.ds(pl.multiple_of(s * ROWS, ROWS), ROWS), :] = value
                else:
                    out_ref[d, pl.ds(pl.multiple_of(s * ROWS, ROWS), ROWS), :] = value

    in_groups(slots, tiles, square.shape[1])
    if last:
        for d in range(out_ref.shape[0]):
            for start in range(0, slots, 8):
                for k in range(ROWS):
                    rows = pl.ds(start * ROWS + k, 8, stride=ROWS)
                    if d in directions:
                        value = refs[4][directions.index(d), rows, :]
                    else:
                        value = done_ref[d, rows, :]
                    out_ref[d, start : start + 8, k * LANES : (k + 1) * LANES] = value


def second_term(directions, own, places, ways, orbs, first, row_blocks, done=None):
    nd, slots = first.shape[:2]
    count = len(directions)
    last = done is not None
    shape = ways[0][0].shape
    rows = (count, slots * ROWS, LANES)
    scratch = [
        pltpu.VMEM((count,) + shape, F32),
        pltpu.VMEM((count, 8, TILE, LANES), F32),
        pltpu.SemaphoreType.DMA((count,)),
    ]
    if last:
        scratch.append(pltpu.VMEM(rows, F32))
    flat = [way for each in ways for way in each]
    others = [first, done] if last else [first]
    specs = [pl.BlockSpec(memory_space=pl.ANY)] * len(flat)
    specs.append(orb_spec(row_blocks, orbs, lambda r, c, p: p[0]))
    specs += [whole(a) for a in others]
    out = jax.ShapeDtypeStruct((nd, slots, ROWS * LANES) if last else rows, F32)
    return call(
        functools.partial(second_kernel, directions, len(ways[0]), last), "second_term",
        [*own, places], [*flat, orbs, *others], specs, out, scratch, slots,
    )


def after(value, other):
    hbm = pl.BlockSpec(memory_space=pl.ANY)
    return pl.pallas_call(
        lambda value_ref, other_ref, out_ref: None,
        out_shape=jax.ShapeDtypeStruct(value.shape, value.dtype),
        in_specs=[hbm, hbm],
        out_specs=hbm,
        input_output_aliases={0: 0},
        name="after",
    )(value, other)


def ring_order(count):
    return list(range(0, count, 2)) + list(range(count - 1, 0, -2))


def row_broadcast(value, row_count, col_count, ratio, held=None):
    ways = [value]
    for k in range(1, row_count):
        parent = k & (k - 1)
        sent = ways[parent]
        if k & 1:
            rows = [[(r, r ^ 1) for r in range(row_count)]] * col_count
        else:
            rows = [[(c // ratio ^ parent, c // ratio ^ k)] for c in range(col_count)]
        if held is not None and parent:
            sent = after(sent, held(ways))
        pairs = [(a * col_count + c, b * col_count + c) for c in range(col_count) for a, b in rows[c]]
        ways.append(lax.ppermute(sent, ("row", "col"), pairs))
    return ways


def local(
    density_tiles,
    tile_ids,
    batch_blocks,
    basis_values,
    grid_weight,
    xc_kernel,
    grid_coord,
    orbitals,
    precond_diag,
    orbital_energy,
):
    row_count = lax.axis_size("row")
    col_count = lax.axis_size("col")
    device_count = row_count * col_count
    own_row = lax.axis_index("row")
    own_col = lax.axis_index("col")
    own_index = own_row * col_count + own_col
    block_count = NB // TILE
    row_blocks = block_count // row_count
    col_blocks = block_count // col_count
    per_range = FB // row_count
    slot_count = tile_ids.shape[0]
    ratio = col_count // row_count
    col_width = col_blocks * TILE
    nd = density_tiles.shape[0]
    nocc = orbitals.shape[1]

    ask = batch_blocks
    match = ask // col_blocks == own_col
    ask_col = jnp.sum(jnp.where(match, ask, 0), axis=1)
    ask_row = lax.dynamic_slice_in_dim(ask, own_row * per_range, per_range, 1)
    wanted = jnp.where(jnp.any(match, axis=1)[:, None], ask_row * block_count + ask_col[:, None], -1)
    hit = wanted.reshape(-1)[:, None] == tile_ids[None, :]
    slots = jnp.max(jnp.where(hit, jnp.arange(slot_count, dtype=jnp.int32)[None, :], -1), axis=1)
    own_cols = lax.dynamic_slice_in_dim(ask, own_index, 1, 0)[0] // col_blocks

    local_rows = tile_ids // block_count - own_row * row_blocks
    local_cols = tile_ids % col_blocks

    order = ring_order(col_count)
    place = [order.index(c) for c in range(col_count)]
    forward = [(order[i], order[(i + 1) % col_count]) for i in range(col_count)]
    backward = [(b, a) for a, b in forward]
    ring = jnp.asarray(order, jnp.int32)
    at = jnp.asarray(place, jnp.int32)[own_col]
    part = own_col % ratio
    half = slot_count // 2
    steps = col_count // 2 - 1

    diag = precond_diag.reshape(row_blocks, ROWS, 2).swapaxes(1, 2).reshape(row_blocks, TILE, 1)
    term_place = jnp.stack([own_row, own_row ^ (own_col // ratio), own_col])

    all_orbitals = lax.all_gather(orbitals, "row", axis=0, tiled=True)
    pad = -slot_count % (8 * LANES)
    ids = jnp.pad(tile_ids, (0, pad)).reshape(-1, LANES).astype(F32)
    picked = pick_tiles(slots, density_tiles, ids, device_count)
    exchange = lambda a: lax.all_to_all(
        a, ("row", "col"), split_axis=0, concat_axis=0, tiled=True
    )
    arrived = exchange(picked)
    listed = lax.dynamic_slice(
        arrived, (own_row * col_count, arrived.shape[1] - ids.shape[0], 0), (col_count,) + ids.shape
    )
    listed = listed.reshape(col_count, -1)[:, :slot_count].astype(jnp.int32)
    listed_rows = listed // block_count - own_row * row_blocks
    listed_cols = listed % col_blocks

    def plan(offsets):
        cols = ring[(at + jnp.asarray(offsets, jnp.int32)) % col_count]
        rows = listed_rows[cols].reshape(-1)
        blocks = listed_cols[cols].reshape(-1)
        return rows, blocks, jnp.append(cols, part)

    near = plan((0, -1, 1))
    far = plan([o for step in range(2, steps + 1) for o in (-step, step)] + [col_count // 2])
    tables = (diag, local_rows, local_cols, term_place)
    arrived, tables = lax.optimization_barrier((arrived, tables))
    diag, local_rows, local_cols, term_place = tables
    built = batch_tiles(
        per_range, col_count, own_cols, arrived, basis_values[0], grid_weight, xc_kernel, grid_coord
    )
    returned = exchange(built)
    hams = add_tiles(slots, returned, slot_count, nd)

    orbs = split_orbitals(all_orbitals, col_count)

    own = (local_rows, local_cols)
    energy = orbital_energy[None]
    send_up = lambda a: lax.ppermute(a, "col", forward)
    send_down = lambda a: lax.ppermute(a, "col", backward)

    ups = [send_up(ham) for ham in hams]
    downs = [send_down(ham) for ham in hams]
    ups[0] = after(ups[0], orbs)
    totals = add_rows([hams, ups, downs], near, orbs, row_blocks, col_blocks)

    early = tuple(range(nd - 1))
    ways = []
    ends = []
    sums = []

    def finished(last_ways):
        sums.append(first_term(own, term_place, ends, diag, energy, orbs, col_blocks))
        sums.append(second_term(early, own, term_place, ways, orbs, sums[0], row_blocks))
        return sums[1]

    for d in range(nd):
        up, down = ups[d], downs[d]
        chunks = []
        for step in range(2, steps + 1):
            if step == 2 and d == nd - 1 or step == 3 and d == 0:
                up, down = after(up, totals[0]), after(down, totals[0])
            if step == 3 and d == nd - 1:
                up, down = after(up, ends[0]), after(down, ends[0])
            up, down = send_up(up), send_down(down)
            chunks += [up, down]
        if d:
            up, down = after(up, ends[d - 1]), after(down, ends[d - 1])
            chunks[-2:] = [up, down]
        chunks += [send_up(up[:half]), send_down(down[half:])]
        total = totals[d]
        if d == nd - 1:
            total = after(total, ways[0][row_count // 2])
        piece, end = response_piece(total, chunks, far, orbs, diag, energy, col_blocks)
        ends.append(end)
        held = None
        if d == nd - 1:
            held = lambda last: sums[1] if sums else finished(last)
        ways.append(row_broadcast(piece, row_count, col_count, ratio, held))
    return second_term((nd - 1,), own, term_place, ways[-1:], orbs, sums[0], row_blocks, sums[1])


def solution(mesh):
    placed = (
        P(None, ("row", "col"), None),
        P(("row", "col")),
        P(),
        P(("row", "col"), None, None),
        P(("row", "col"), None),
        P(("row", "col"), None),
        P(None, ("row", "col"), None),
        P("row", None),
        P("row"),
        P(),
    )
    return jax.shard_map(
        local, mesh=mesh, in_specs=placed, out_specs=P(None, ("row", "col"), None), check_vma=False
    )
```

```python
import functools

import jax
import jax.numpy as jnp
from jax import lax
from jax.experimental import pallas as pl
from jax.experimental.pallas import tpu as pltpu
from jax.sharding import PartitionSpec as P

NB = 8192
TILE = 64
FB = 8
LANES = 2 * TILE
ROWS = TILE * TILE // LANES
F32 = jnp.float32
BF16 = jnp.bfloat16
NT = (((1,), (1,)), ((), ()))


def split(value):
    high = value.astype(BF16)
    return high, (value - high.astype(F32)).astype(BF16)


def dot(a, b):
    return jnp.dot(a, b, preferred_element_type=F32)


def dot_nt(a, b):
    return lax.dot_general(a, b, NT, preferred_element_type=F32)


def low_lanes(shape):
    return lax.broadcasted_iota(jnp.int32, shape, len(shape) - 1) < TILE


def params(mib):
    return pltpu.CompilerParams(vmem_limit_bytes=mib * 2**20)


VMEM = pl.BlockSpec(memory_space=pltpu.VMEM)
SMEM = pl.BlockSpec(memory_space=pltpu.SMEM)


def in_groups(count, body, group=16):
    if count % group:
        group = 1

    def step(g, carry):
        body([g * group + u for u in range(group)])
        return carry

    lax.fori_loop(0, count // group, step, 0)


def pick_kernel(slot_ref, tiles_ref, ids_ref, out_ref, rows):
    nd, slots, area = tiles_ref.shape
    per_range = slot_ref.shape[0] // out_ref.shape[0]
    for d in range(nd):
        for start in range(0, slots, 8):
            for k in range(area // LANES):
                rows[d, pl.ds(start * ROWS + k, 8, stride=ROWS), :] = tiles_ref[
                    d, start : start + 8, k * LANES : (k + 1) * LANES
                ]

    def device(index):
        for n in index:
            for k in range(per_range):
                slot = slot_ref[n * per_range + k]
                first = pl.multiple_of(jnp.maximum(slot, 0) * ROWS, ROWS)
                for d in range(nd):
                    out_ref[n, (k * nd + d) * ROWS : (k * nd + d + 1) * ROWS] = jnp.where(
                        slot >= 0, rows[d, pl.ds(first, ROWS), :], 0.0
                    )
            out_ref[n, per_range * nd * ROWS :] = ids_ref[...]

    in_groups(out_ref.shape[0], device, 2)


def pick_tiles(slots, tiles, ids, device_count):
    nd, count, area = tiles.shape
    rows = slots.shape[0] // device_count * nd * ROWS + ids.shape[0]
    return pl.pallas_call(
        pick_kernel,
        out_shape=jax.ShapeDtypeStruct((device_count, rows, LANES), F32),
        in_specs=[SMEM, VMEM, VMEM],
        out_specs=VMEM,
        scratch_shapes=[pltpu.VMEM((nd, count * ROWS, LANES), F32)],
        compiler_params=params(32),
        name="pick_tiles",
    )(slots, tiles, ids)


def batch_kernel(
    per_range, col_count, col_ref, tiles_ref, basis_ref, weight_ref, xc_ref, coord_ref, out_ref,
    bh, bl, wh, wl, square,
):
    nd = coord_ref.shape[0]
    width, pts = basis_ref.shape
    low = low_lanes((ROWS, LANES))
    if col_count > FB:
        out_ref[...] = jnp.zeros(out_ref.shape, F32)

    def place(i, j, d):
        owner = (i // per_range) * col_count + col_ref[j]
        return owner, pl.ds(pl.multiple_of((i % per_range * nd + d) * ROWS, ROWS), ROWS)

    high, rest = split(basis_ref[...])
    bh[...] = high
    bl[...] = rest

    def direction(d, carry):
        for i in range(FB):
            for jj in range(FB // 2):
                first = tiles_ref[place(i, 2 * jj, d)]
                second = tiles_ref[place(i, 2 * jj + 1, d)]
                square[jj, pl.ds(i * TILE, ROWS, stride=2), :] = jnp.where(
                    low, first, pltpu.roll(second, TILE, 1)
                )
                square[jj, pl.ds(i * TILE + 1, ROWS, stride=2), :] = jnp.where(
                    low, pltpu.roll(first, TILE, 1), second
                )
        eh, el = split(jnp.concatenate([square[jj] for jj in range(FB // 2)], axis=1))
        piece = 256
        for start in range(0, pts, piece):
            cols = slice(start, start + piece)
            projected = dot(eh, bh[:, cols]) + dot(eh, bl[:, cols]) + dot(el, bh[:, cols])
            values = basis_ref[:, cols]
            response = jnp.sum(values * projected, axis=0, keepdims=True)
            potential = xc_ref[:, cols] * response + coord_ref[d, :, cols]
            weighted = values * (weight_ref[:, cols] * potential)
            high, rest = split(weighted)
            wh[:, cols] = high
            wl[:, cols] = rest
        for start in range(0, width, piece):
            rows = slice(start, start + piece)
            value = (
                dot_nt(wh[...], bh[rows]) + dot_nt(wh[...], bl[rows]) + dot_nt(wl[...], bh[rows])
            )
            for lane in range(0, piece, LANES):
                square[(start + lane) // LANES] = value[:, lane : lane + LANES]
        for i in range(FB):
            for jj in range(FB // 2):
                even = square[jj, pl.ds(i * TILE, ROWS, stride=2), :]
                odd = square[jj, pl.ds(i * TILE + 1, ROWS, stride=2), :]
                out_ref[place(i, 2 * jj, d)] = jnp.where(low, even, pltpu.roll(odd, TILE, 1))
                out_ref[place(i, 2 * jj + 1, d)] = jnp.where(low, pltpu.roll(even, TILE, 1), odd)
        return carry

    lax.fori_loop(0, nd, direction, 0)


def batch_tiles(per_range, col_count, cols, tiles, basis, weight, xc, coord):
    width, pts = basis.shape
    return pl.pallas_call(
        functools.partial(batch_kernel, per_range, col_count),
        out_shape=jax.ShapeDtypeStruct(
            (tiles.shape[0], per_range * coord.shape[0] * ROWS, LANES), F32
        ),
        in_specs=[SMEM] + [VMEM] * 5,
        out_specs=VMEM,
        scratch_shapes=[
            pltpu.VMEM((width, pts), BF16),
            pltpu.VMEM((width, pts), BF16),
            pltpu.VMEM((width, pts), BF16),
            pltpu.VMEM((width, pts), BF16),
            pltpu.VMEM((width // LANES, width, LANES), F32),
        ],
        compiler_params=params(48),
        name="batch_tiles",
    )(cols, tiles, basis, weight, xc, coord)


def add_kernel(slot_ref, tiles_ref, out_ref):
    nd = out_ref.shape[0]
    per_range = slot_ref.shape[0] // tiles_ref.shape[0]
    out_ref[...] = jnp.zeros(out_ref.shape, F32)

    def step(n, carry):
        for k in range(per_range):
            slot = slot_ref[n * per_range + k]

            @pl.when(slot >= 0)
            def _(slot=slot, k=k):
                for d in range(nd):
                    start = (k * nd + d) * ROWS
                    out_ref[d, slot] += tiles_ref[n, start : start + ROWS]

        return carry

    lax.fori_loop(0, tiles_ref.shape[0], step, 0)


def add_tiles(slots, tiles, slot_count, nd):
    return pl.pallas_call(
        add_kernel,
        out_shape=jax.ShapeDtypeStruct((nd, slot_count, ROWS, LANES), F32),
        in_specs=[SMEM, VMEM],
        out_specs=VMEM,
        compiler_params=params(32),
        name="add_tiles",
    )(slots, tiles)


def split_kernel(orb_ref, out_ref, mark_ref):
    mark_ref[...] = jnp.zeros(mark_ref.shape, F32)

    def blocks(index):
        for b in index:
            high, rest = split(orb_ref[pl.ds(pl.multiple_of(b * TILE, TILE), TILE), :])
            out_ref[b, :TILE] = high
            out_ref[b, TILE:] = rest

    in_groups(out_ref.shape[0], blocks, 2)


def split_orbitals(orbitals, parts):
    count, nocc = orbitals.shape
    return pl.pallas_call(
        split_kernel,
        out_shape=(
            jax.ShapeDtypeStruct((count // TILE, 2 * TILE, nocc), BF16),
            jax.ShapeDtypeStruct((8, LANES), F32),
        ),
        grid=(parts,),
        in_specs=[pl.BlockSpec((count // parts, nocc), lambda g: (g, 0))],
        out_specs=(
            pl.BlockSpec((count // parts // TILE, 2 * TILE, nocc), lambda g: (g, 0, 0)),
            pl.BlockSpec((8, LANES), lambda g: (0, 0)),
        ),
        compiler_params=params(60),
        cost_estimate=pl.CostEstimate(
            flops=0, bytes_accessed=8 * count * nocc, transcendentals=0
        ),
        name="split_orbitals",
    )(orbitals)


def accumulate(chunk, orb, row_id, col_id, offset, sums):
    low = low_lanes((ROWS, LANES))
    nd = len(sums)

    def tiles(index):
        products = []
        for s in index:
            left = []
            for d in range(nd):
                tile = chunk[d, s]
                turned = pltpu.roll(tile, TILE, 1)
                left += [split(jnp.where(low, tile, turned)), split(jnp.where(low, turned, tile))]
            pair = orb[col_id[offset + s]]
            if nd > 1:
                left = jnp.concatenate([jnp.concatenate(parts, axis=1) for parts in left], axis=0)
                products.append(dot(left, jnp.concatenate([pair, pair], axis=0)))
            else:
                left = jnp.concatenate([parts[k] for k in range(2) for parts in left], axis=0)
                product = dot(left, pair)
                products.append(product[:TILE] + product[TILE:])
        for s, product in zip(index, products):
            block = row_id[offset + s]
            for d in range(nd):
                sums[d][block] += product[d * TILE : (d + 1) * TILE]

    in_groups(chunk.shape[1], tiles, 16 if nd > 1 else 32)


def whole(a):
    return pl.BlockSpec(a.shape, lambda g, *_, n=len(a.shape): (0,) * n)


def orb_spec(blocks, orbs, which):
    return pl.BlockSpec((blocks,) + orbs.shape[1:], lambda g, *t: (which(*t), 0, 0))


def call(kernel, name, tables, args, specs, out, scratch, products, mib=60):
    single = not isinstance(out, (tuple, list))
    return pl.pallas_call(
        kernel,
        out_shape=out,
        grid_spec=pltpu.PrefetchScalarGridSpec(
            num_scalar_prefetch=len(tables),
            grid=(1,),
            in_specs=specs,
            out_specs=whole(out) if single else [whole(o) for o in out],
            scratch_shapes=scratch,
        ),
        compiler_params=params(mib),
        cost_estimate=pl.CostEstimate(
            flops=products * 100_000_000, bytes_accessed=2**23, transcendentals=0
        ),
        name=name,
    )(*tables, *args)


def rows_kernel(count, nd, fresh, row_id, col_id, place_ref, *refs):
    chunks, orbs, refs = refs[:count], refs[count : 2 * count], refs[2 * count :]
    if fresh:
        sums = refs
        for total in sums:
            total[...] = jnp.zeros(total.shape, F32)
    else:
        before, sums, sem = refs[:nd], refs[nd : 2 * nd], refs[2 * nd]
        loads = [pltpu.make_async_copy(before[d], sums[d], sem.at[d]) for d in range(nd)]
        for load in loads:
            load.start()
        for load in loads:
            load.wait()
    offset = 0
    for chunk, orb in zip(chunks, orbs):
        accumulate(chunk, orb, row_id, col_id, offset, sums)
        offset += chunk.shape[1]


def add_rows(totals, chunks, where, orbs, row_blocks, col_blocks):
    count = len(chunks)
    nd, slots = chunks[0].shape[:2]
    args = list(chunks)
    specs = [whole(c) for c in args]
    specs += [orb_spec(col_blocks, orbs, lambda r, c, p, k=k: p[k]) for k in range(count)]
    args += [orbs] * count
    scratch = []
    if totals is not None:
        specs += [pl.BlockSpec(memory_space=pl.ANY)] * nd
        args += totals
        scratch.append(pltpu.SemaphoreType.DMA((nd,)))
    out = jax.ShapeDtypeStruct((row_blocks, TILE, orbs.shape[2]), F32)
    return call(
        functools.partial(rows_kernel, count, nd, totals is None), "add_rows", where, args, specs,
        [out] * nd, scratch, count * slots,
    )


def piece_kernel(count, halves, row_id, col_id, place_ref, *refs):
    chunks, refs = refs[:count], refs[count:]
    orbs_ref, in_ref, diag_ref, energy_ref, piece_ref, total_ref, sums, square, chunk_buf, orb_buf = refs[:10]
    sem, chunk_sem, orb_sem = refs[10:]
    ranges = count - halves
    col_blocks = orb_buf.shape[1]
    load = pltpu.make_async_copy(in_ref, sums, sem)
    load.start()
    moves = []
    for k in range(count):
        size = chunks[k].shape[1]
        start = chunks[0].shape[1] if halves and k == count - 1 else 0
        start = start // 2
        target = chunk_buf.at[min(k, ranges - 1), pl.ds(start, size)]
        moves.append(pltpu.make_async_copy(chunks[k].at[0], target, chunk_sem.at[k]))
        moves[-1].start()
        if k < ranges:
            source = orbs_ref.at[pl.ds(place_ref[k] * col_blocks, col_blocks)]
            moves.append(pltpu.make_async_copy(source, orb_buf.at[k], orb_sem.at[k]))
            moves[-1].start()
    load.wait()
    offset = 0
    for k in range(ranges):
        for move in moves[2 * k : 2 * k + 2 + (halves if k == ranges - 1 else 0)]:
            move.wait()
        accumulate(chunk_buf.at[pl.ds(k, 1)], orb_buf.at[k], row_id, col_id, offset, [sums])
        offset += chunk_buf.shape[1]
    store = pltpu.make_async_copy(sums, total_ref, sem)
    store.start()
    first = place_ref[ranges] * piece_ref.shape[0]
    energy = energy_ref[...]

    def blocks(index):
        for b in index:
            value = sums[first + b] * (-1.0 / (diag_ref[first + b] - energy))
            for k in range(square.shape[1]):
                lanes = slice(k * LANES, (k + 1) * LANES)
                for parity in range(2):
                    square[b % 4, k, pl.ds(parity, ROWS, stride=2), :] = value[
                        parity * ROWS : (parity + 1) * ROWS, lanes
                    ]
                piece_ref[b, :, lanes] = square[b % 4, k]

    in_groups(piece_ref.shape[0], blocks, 4)
    store.wait()


def response_piece(total, chunks, where, orbs, diag, energy, col_blocks):
    count = len(chunks)
    halves = int(chunks[-1].shape != chunks[0].shape)
    ranges = count - halves
    nocc = orbs.shape[2]
    hbm = pl.BlockSpec(memory_space=pl.ANY)
    piece = jax.ShapeDtypeStruct((col_blocks, TILE, nocc), F32)
    return pl.pallas_call(
        functools.partial(piece_kernel, count, halves),
        out_shape=(piece, jax.ShapeDtypeStruct(total.shape, F32)),
        grid_spec=pltpu.PrefetchScalarGridSpec(
            num_scalar_prefetch=3,
            grid=(1,),
            in_specs=[hbm] * (count + 2) + [whole(diag), whole(energy)],
            out_specs=(whole(piece), hbm),
            scratch_shapes=[
                pltpu.VMEM(total.shape, F32),
                pltpu.VMEM((4, nocc // LANES, TILE, LANES), F32),
                pltpu.VMEM((ranges,) + chunks[0].shape[1:], F32),
                pltpu.VMEM((ranges, col_blocks) + orbs.shape[1:], BF16),
                pltpu.SemaphoreType.DMA,
                pltpu.SemaphoreType.DMA((count,)),
                pltpu.SemaphoreType.DMA((ranges,)),
            ],
        ),
        compiler_params=params(60),
        cost_estimate=pl.CostEstimate(
            flops=20_000_000_000, bytes_accessed=2**23, transcendentals=0
        ),
        name="response_piece",
    )(*where, *chunks, orbs, total, diag, energy)


def first_tiles(totals, diag_ref, energy_ref, orb_ref, row_id, col_id, out_ref):
    low = low_lanes((ROWS, LANES))

    def tiles(index):
        for s in index:
            block = row_id[s]
            inverse = -1.0 / (diag_ref[block] - energy_ref[...])
            left = [part for total in totals for part in split(total[block] * inverse)]
            value = dot_nt(jnp.concatenate(left, axis=0), orb_ref[col_id[s]])
            for d in range(len(totals)):
                start = 2 * d * TILE
                tile = value[start : start + TILE] + value[start + TILE : start + 2 * TILE]
                tile = tile + pltpu.roll(tile, TILE, 1)
                rows = pl.ds(pl.multiple_of(s * ROWS, ROWS), ROWS)
                out_ref[d, rows, :] = jnp.where(low, tile[:ROWS], tile[ROWS:])

    in_groups(out_ref.shape[1] // ROWS, tiles, 8)


def second_tiles(x_ref, orb_ref, row_id, col_id, square, read, write):
    low = low_lanes((ROWS, LANES))
    count = x_ref.shape[0]

    def tiles(index):
        for u, s in enumerate(index):
            right = [part for d in range(count) for part in split(x_ref[d, col_id[s]])]
            value = dot_nt(orb_ref[row_id[s]], jnp.concatenate(right, axis=0))
            value = value[:TILE] + value[TILE:]
            for d in range(count):
                tile = value[:, d * LANES : (d + 1) * LANES]
                square[d, u] = tile + pltpu.roll(tile, TILE, 1)
        for u, s in enumerate(index):
            rows = pl.ds(pl.multiple_of(s * ROWS, ROWS), ROWS)
            for d in range(count):
                even = square[d, u, pl.ds(0, ROWS, stride=2), :]
                odd = square[d, u, pl.ds(1, ROWS, stride=2), :]
                write(d, rows, read(d, rows) + jnp.where(low, even, odd))

    in_groups(row_id.shape[0], tiles, square.shape[1])


def fetch(place_ref, ways, x_ref, sem):
    for k, way in enumerate(ways):

        @pl.when(place_ref[1] == k)
        def _(way=way):
            pltpu.make_async_copy(way, x_ref, sem).start()

    return pltpu.make_async_copy(ways[0], x_ref, sem).wait


def early_kernel(nd, way_count, row_id, col_id, place_ref, *refs):
    ways = [refs[d * way_count : (d + 1) * way_count] for d in range(nd - 1)]
    refs = refs[(nd - 1) * way_count :]
    totals, refs = refs[:nd], refs[nd:]
    diag_ref, energy_ref, orb_cols, orb_rows, out_ref, x_ref, square, sem = refs
    waits = [fetch(place_ref, ways[d], x_ref.at[d], sem.at[d]) for d in range(nd - 1)]
    first_tiles(totals, diag_ref, energy_ref, orb_cols, row_id, col_id, out_ref)
    for wait in waits:
        wait()

    def write(d, rows, value):
        out_ref[d, rows, :] = value

    second_tiles(
        x_ref, orb_rows, row_id, col_id, square, lambda d, rows: out_ref[d, rows, :], write
    )


def early_terms(own, places, ways, totals, diag, energy, orbs, row_blocks, col_blocks):
    nd, slots = len(totals), own[0].shape[0]
    shape = ways[0][0].shape
    flat = [way for each in ways for way in each]
    specs = [pl.BlockSpec(memory_space=pl.ANY)] * len(flat)
    specs += [whole(a) for a in [*totals, diag, energy]]
    specs.append(orb_spec(col_blocks, orbs, lambda r, c, p: p[2]))
    specs.append(orb_spec(row_blocks, orbs, lambda r, c, p: p[0]))
    return call(
        functools.partial(early_kernel, nd, len(ways[0])), "early_terms", [*own, places],
        [*flat, *totals, diag, energy, orbs, orbs], specs,
        jax.ShapeDtypeStruct((nd, slots * ROWS, LANES), F32),
        [
            pltpu.VMEM((nd - 1,) + shape, F32),
            pltpu.VMEM((nd - 1, 8, TILE, LANES), F32),
            pltpu.SemaphoreType.DMA((nd - 1,)),
        ],
        1,
    )


def last_kernel(way_count, row_id, col_id, place_ref, *refs):
    ways, refs = refs[:way_count], refs[way_count:]
    orb_rows, done_ref, out_ref, x_ref, square, rows_ref, sem = refs
    wait = fetch(place_ref, ways, x_ref.at[0], sem)
    nd, slots, area = out_ref.shape

    def layout(d, source):
        for start in range(0, slots, 8):
            for k in range(area // LANES):
                out_ref[d, start : start + 8, k * LANES : (k + 1) * LANES] = source[
                    pl.ds(start * ROWS + k, 8, stride=ROWS), :
                ]

    for d in range(nd - 1):
        layout(d, done_ref.at[d])
    wait()

    def write(d, rows, value):
        rows_ref[rows, :] = value

    second_tiles(
        x_ref, orb_rows, row_id, col_id, square, lambda d, rows: done_ref[nd - 1, rows, :], write
    )
    layout(nd - 1, rows_ref)


def last_terms(own, places, ways, done, orbs, row_blocks):
    slots = own[0].shape[0]
    nd = done.shape[0]
    specs = [pl.BlockSpec(memory_space=pl.ANY)] * len(ways)
    specs += [orb_spec(row_blocks, orbs, lambda r, c, p: p[0]), whole(done)]
    return call(
        functools.partial(last_kernel, len(ways)), "last_terms", [*own, places],
        [*ways, orbs, done], specs,
        jax.ShapeDtypeStruct((nd, slots, ROWS * LANES), F32),
        [
            pltpu.VMEM((1,) + ways[0].shape, F32),
            pltpu.VMEM((1, 8, TILE, LANES), F32),
            pltpu.VMEM((slots * ROWS, LANES), F32),
            pltpu.SemaphoreType.DMA,
        ],
        slots,
    )


def tie(values, others=()):
    hbm = pl.BlockSpec(memory_space=pl.ANY)
    count = len(values)
    return pl.pallas_call(
        lambda *refs: None,
        out_shape=[jax.ShapeDtypeStruct(v.shape, v.dtype) for v in values],
        in_specs=[hbm] * (count + len(others)),
        out_specs=[hbm] * count,
        input_output_aliases={k: k for k in range(count)},
        name="tie",
    )(*values, *others)


def ring_order(count):
    return list(range(0, count, 2)) + list(range(count - 1, 0, -2))


def row_broadcast(value, row_count, col_count, ratio, held=None):
    def send(k):
        parent = k & (k - 1)
        if k & 1:
            rows = [[(r, r ^ 1) for r in range(row_count)]] * col_count
        else:
            rows = [[(c // ratio ^ parent, c // ratio ^ k)] for c in range(col_count)]
        pairs = [(a * col_count + c, b * col_count + c) for c in range(col_count) for a, b in rows[c]]
        return lax.ppermute(ways[parent], ("row", "col"), pairs)

    ways = [value] + [None] * (row_count - 1)
    for k in range(2, row_count, 2):
        ways[k] = send(k)
    if held is not None:
        mark = held()
        for k in range(2, row_count, 2):
            ways[k] = tie([ways[k]], [mark])[0]
    for k in range(1, row_count, 2):
        ways[k] = send(k)
    return ways


def local(
    density_tiles,
    tile_ids,
    batch_blocks,
    basis_values,
    grid_weight,
    xc_kernel,
    grid_coord,
    orbitals,
    precond_diag,
    orbital_energy,
):
    row_count = lax.axis_size("row")
    col_count = lax.axis_size("col")
    device_count = row_count * col_count
    own_row = lax.axis_index("row")
    own_col = lax.axis_index("col")
    own_index = own_row * col_count + own_col
    block_count = NB // TILE
    row_blocks = block_count // row_count
    col_blocks = block_count // col_count
    per_range = FB // row_count
    slot_count = tile_ids.shape[0]
    ratio = col_count // row_count
    col_width = col_blocks * TILE
    nd = density_tiles.shape[0]
    nocc = orbitals.shape[1]

    ask = batch_blocks
    match = ask // col_blocks == own_col
    ask_col = jnp.sum(jnp.where(match, ask, 0), axis=1)
    ask_row = lax.dynamic_slice_in_dim(ask, own_row * per_range, per_range, 1)
    wanted = jnp.where(jnp.any(match, axis=1)[:, None], ask_row * block_count + ask_col[:, None], -1)
    hit = wanted.reshape(-1)[:, None] == tile_ids[None, :]
    slots = jnp.max(jnp.where(hit, jnp.arange(slot_count, dtype=jnp.int32)[None, :], -1), axis=1)
    own_cols = lax.dynamic_slice_in_dim(ask, own_index, 1, 0)[0] // col_blocks

    local_rows = tile_ids // block_count - own_row * row_blocks
    local_cols = tile_ids % col_blocks

    order = ring_order(col_count)
    place = [order.index(c) for c in range(col_count)]
    forward = [(order[i], order[(i + 1) % col_count]) for i in range(col_count)]
    backward = [(b, a) for a, b in forward]
    ring = jnp.asarray(order, jnp.int32)
    at = jnp.asarray(place, jnp.int32)[own_col]
    part = own_col % ratio
    half = slot_count // 2
    steps = col_count // 2 - 1

    diag = precond_diag.reshape(row_blocks, ROWS, 2).swapaxes(1, 2).reshape(row_blocks, TILE, 1)
    term_place = jnp.stack([own_row, own_row ^ (own_col // ratio), own_col])

    all_orbitals = lax.all_gather(orbitals, "row", axis=0, tiled=True)
    pad = -slot_count % (8 * LANES)
    ids = jnp.pad(tile_ids, (0, pad)).reshape(-1, LANES).astype(F32)
    picked = pick_tiles(slots, density_tiles, ids, device_count)
    exchange = lambda a: lax.all_to_all(
        a, ("row", "col"), split_axis=0, concat_axis=0, tiled=True
    )
    arrived = exchange(picked)
    listed = lax.dynamic_slice(
        arrived, (own_row * col_count, arrived.shape[1] - ids.shape[0], 0), (col_count,) + ids.shape
    )
    listed = listed.reshape(col_count, -1)[:, :slot_count].astype(jnp.int32)
    listed_rows = listed // block_count - own_row * row_blocks
    listed_cols = listed % col_blocks

    def plan(offsets):
        cols = ring[(at + jnp.asarray(offsets, jnp.int32)) % col_count]
        rows = listed_rows[cols].reshape(-1)
        blocks = listed_cols[cols].reshape(-1)
        return rows, blocks, jnp.append(cols, part)

    plans = [plan((0, -1, 1))]
    plans += [plan((-step, step)) for step in range(2, steps)]
    plans[-1:] = [plan((-steps + 1, steps - 1, -steps, steps, col_count // 2))]
    tables = (diag, local_rows, local_cols, term_place)
    arrived, tables = lax.optimization_barrier((arrived, tables))
    diag, local_rows, local_cols, term_place = tables
    built = batch_tiles(
        per_range, col_count, own_cols, arrived, basis_values[0], grid_weight, xc_kernel, grid_coord
    )
    returned = exchange(built)
    ham = add_tiles(slots, returned, slot_count, nd)

    orbs, mark = split_orbitals(all_orbitals, col_count)

    own = (local_rows, local_cols)
    energy = orbital_energy[None]
    send_up = lambda a: lax.ppermute(a, "col", forward)
    send_down = lambda a: lax.ppermute(a, "col", backward)

    marks = [mark, diag, *(table for where in plans for table in where)]
    up, down = tie([send_up(ham), send_down(ham)], marks)
    totals = None
    for step in range(2, steps):
        chunks = [ham, up, down] if totals is None else [up, down]
        sums = add_rows(totals, chunks, plans[step - 2], orbs, row_blocks, col_blocks)
        up, down, *totals = tie([send_up(up), send_down(down), *sums])

    def go(d):
        ups[d], downs[d] = send_up(ups[d]), send_down(downs[d])

    def opposite(d):
        return [send_up(ups[d][:, :half]), send_down(downs[d][:, half:])]

    def finish(d, ends):
        chunks = [up2[d], down2[d], ups[d], downs[d], *ends]
        return response_piece(totals[d], chunks, plans[-1], orbs, diag, energy, col_blocks)

    def spread(piece, held=None):
        return row_broadcast(piece, row_count, col_count, ratio, held)

    def wait(value, moving, *others):
        kept = [a[k] for a in (ups, downs, totals) for k in moving]
        held = tie([*value, *kept], others)
        kept = list(held[len(value) :])
        for a in (ups, downs, totals):
            for k in moving:
                a[k] = kept.pop(0)
        return list(held[: len(value)])

    ups = [up[d : d + 1] for d in range(nd)]
    downs = [down[d : d + 1] for d in range(nd)]
    up2, down2 = list(ups), list(downs)
    everything = range(nd)
    go(0)
    wait([], everything)
    ends = wait(opposite(0), everything)
    for d in everything[1:]:
        go(d)
    pieces, sums, ways = [], [], []
    for d in everything:
        if d == nd - 1:
            totals[d] = tie([totals[d]], [ways[0][row_count // 2]])[0]
        piece, total = finish(d, ends)
        pieces.append(piece)
        sums.append(total)
        if d == 0:
            ways.append(spread(piece))
            wait([], [1], total)
            ends = wait(opposite(1), everything[1:])
        elif d < nd - 1:
            ends = wait(opposite(d + 1), [d + 1], total)
    for d in range(1, nd - 1):
        ways.append(spread(pieces[d], lambda: sums[-1]))
    piece = tie([piece], [way[row_count // 2] for way in ways])[0]
    done = early_terms(own, term_place, ways, sums, diag, energy, orbs, row_blocks, col_blocks)
    ways.append(spread(piece, lambda: done))
    return last_terms(own, term_place, ways[-1], done, orbs, row_blocks)


def solution(mesh):
    placed = (
        P(None, ("row", "col"), None),
        P(("row", "col")),
        P(),
        P(("row", "col"), None, None),
        P(("row", "col"), None),
        P(("row", "col"), None),
        P(None, ("row", "col"), None),
        P("row", None),
        P("row"),
        P(),
    )
    return jax.shard_map(
        local, mesh=mesh, in_specs=placed, out_specs=P(None, ("row", "col"), None), check_vma=False
    )
```

```python
import functools

import jax
import jax.numpy as jnp
from jax import lax
from jax.experimental import pallas as pl
from jax.experimental.pallas import tpu as pltpu
from jax.sharding import PartitionSpec as P

NB = 8192
TILE = 64
FB = 8
LANES = 2 * TILE
ROWS = TILE * TILE // LANES
F32 = jnp.float32
BF16 = jnp.bfloat16
NT = (((1,), (1,)), ((), ()))


def split(value):
    high = value.astype(BF16)
    return high, (value - high.astype(F32)).astype(BF16)


def dot(a, b):
    return jnp.dot(a, b, preferred_element_type=F32)


def dot_nt(a, b):
    return lax.dot_general(a, b, NT, preferred_element_type=F32)


def low_lanes(shape):
    return lax.broadcasted_iota(jnp.int32, shape, len(shape) - 1) < TILE


def params(mib):
    return pltpu.CompilerParams(vmem_limit_bytes=mib * 2**20)


VMEM = pl.BlockSpec(memory_space=pltpu.VMEM)
SMEM = pl.BlockSpec(memory_space=pltpu.SMEM)


def in_groups(count, body, group=16):
    if count % group:
        group = 1

    def step(g, carry):
        body([g * group + u for u in range(group)])
        return carry

    lax.fori_loop(0, count // group, step, 0)


def pick_kernel(slot_ref, tiles_ref, ids_ref, out_ref, rows):
    nd, slots, area = tiles_ref.shape
    per_range = slot_ref.shape[0] // out_ref.shape[0]
    for d in range(nd):
        for start in range(0, slots, 8):
            for k in range(area // LANES):
                rows[d, pl.ds(start * ROWS + k, 8, stride=ROWS), :] = tiles_ref[
                    d, start : start + 8, k * LANES : (k + 1) * LANES
                ]

    def device(index):
        for n in index:
            for k in range(per_range):
                slot = slot_ref[n * per_range + k]
                first = pl.multiple_of(jnp.maximum(slot, 0) * ROWS, ROWS)
                for d in range(nd):
                    out_ref[n, (k * nd + d) * ROWS : (k * nd + d + 1) * ROWS] = jnp.where(
                        slot >= 0, rows[d, pl.ds(first, ROWS), :], 0.0
                    )
            out_ref[n, per_range * nd * ROWS :] = ids_ref[...]

    in_groups(out_ref.shape[0], device, 2)


def pick_tiles(slots, tiles, ids, device_count):
    nd, count, area = tiles.shape
    rows = slots.shape[0] // device_count * nd * ROWS + ids.shape[0]
    return pl.pallas_call(
        pick_kernel,
        out_shape=jax.ShapeDtypeStruct((device_count, rows, LANES), F32),
        in_specs=[SMEM, VMEM, VMEM],
        out_specs=VMEM,
        scratch_shapes=[pltpu.VMEM((nd, count * ROWS, LANES), F32)],
        compiler_params=params(32),
        name="pick_tiles",
    )(slots, tiles, ids)


def batch_kernel(
    per_range, col_count, col_ref, tiles_ref, basis_ref, weight_ref, xc_ref, coord_ref, out_ref,
    bh, bl, wh, wl, square,
):
    nd = coord_ref.shape[0]
    width, pts = basis_ref.shape
    low = low_lanes((ROWS, LANES))
    if col_count > FB:
        out_ref[...] = jnp.zeros(out_ref.shape, F32)

    def place(i, j, d):
        owner = (i // per_range) * col_count + col_ref[j]
        return owner, pl.ds(pl.multiple_of((i % per_range * nd + d) * ROWS, ROWS), ROWS)

    high, rest = split(basis_ref[...])
    bh[...] = high
    bl[...] = rest

    def direction(d, carry):
        for i in range(FB):
            for jj in range(FB // 2):
                first = tiles_ref[place(i, 2 * jj, d)]
                second = tiles_ref[place(i, 2 * jj + 1, d)]
                square[jj, pl.ds(i * TILE, ROWS, stride=2), :] = jnp.where(
                    low, first, pltpu.roll(second, TILE, 1)
                )
                square[jj, pl.ds(i * TILE + 1, ROWS, stride=2), :] = jnp.where(
                    low, pltpu.roll(first, TILE, 1), second
                )
        eh, el = split(jnp.concatenate([square[jj] for jj in range(FB // 2)], axis=1))
        piece = 256
        for start in range(0, pts, piece):
            cols = slice(start, start + piece)
            projected = dot(eh, bh[:, cols]) + dot(eh, bl[:, cols]) + dot(el, bh[:, cols])
            values = basis_ref[:, cols]
            response = jnp.sum(values * projected, axis=0, keepdims=True)
            potential = xc_ref[:, cols] * response + coord_ref[d, :, cols]
            weighted = values * (weight_ref[:, cols] * potential)
            high, rest = split(weighted)
            wh[:, cols] = high
            wl[:, cols] = rest
        for start in range(0, width, piece):
            rows = slice(start, start + piece)
            value = (
                dot_nt(wh[...], bh[rows]) + dot_nt(wh[...], bl[rows]) + dot_nt(wl[...], bh[rows])
            )
            for lane in range(0, piece, LANES):
                square[(start + lane) // LANES] = value[:, lane : lane + LANES]
        for i in range(FB):
            for jj in range(FB // 2):
                even = square[jj, pl.ds(i * TILE, ROWS, stride=2), :]
                odd = square[jj, pl.ds(i * TILE + 1, ROWS, stride=2), :]
                out_ref[place(i, 2 * jj, d)] = jnp.where(low, even, pltpu.roll(odd, TILE, 1))
                out_ref[place(i, 2 * jj + 1, d)] = jnp.where(low, pltpu.roll(even, TILE, 1), odd)
        return carry

    lax.fori_loop(0, nd, direction, 0)


def batch_tiles(per_range, col_count, cols, tiles, basis, weight, xc, coord):
    width, pts = basis.shape
    return pl.pallas_call(
        functools.partial(batch_kernel, per_range, col_count),
        out_shape=jax.ShapeDtypeStruct(
            (tiles.shape[0], per_range * coord.shape[0] * ROWS, LANES), F32
        ),
        in_specs=[SMEM] + [VMEM] * 5,
        out_specs=VMEM,
        scratch_shapes=[
            pltpu.VMEM((width, pts), BF16),
            pltpu.VMEM((width, pts), BF16),
            pltpu.VMEM((width, pts), BF16),
            pltpu.VMEM((width, pts), BF16),
            pltpu.VMEM((width // LANES, width, LANES), F32),
        ],
        compiler_params=params(48),
        name="batch_tiles",
    )(cols, tiles, basis, weight, xc, coord)


def add_kernel(slot_ref, tiles_ref, head_ref, rest_ref):
    nd = head_ref.shape[0] + 1
    per_range = slot_ref.shape[0] // tiles_ref.shape[0]
    head_ref[...] = jnp.zeros(head_ref.shape, F32)
    rest_ref[...] = jnp.zeros(rest_ref.shape, F32)

    def step(n, carry):
        for k in range(per_range):
            slot = slot_ref[n * per_range + k]

            @pl.when(slot >= 0)
            def _(slot=slot, k=k):
                for d in range(nd):
                    start = (k * nd + d) * ROWS
                    ref, at = (head_ref, d) if d < nd - 1 else (rest_ref, 0)
                    ref[at, slot] += tiles_ref[n, start : start + ROWS]

        return carry

    lax.fori_loop(0, tiles_ref.shape[0], step, 0)


def add_tiles(slots, tiles, slot_count, nd):
    return pl.pallas_call(
        add_kernel,
        out_shape=[jax.ShapeDtypeStruct((n, slot_count, ROWS, LANES), F32) for n in (nd - 1, 1)],
        in_specs=[SMEM, VMEM],
        out_specs=[VMEM, VMEM],
        compiler_params=params(32),
        name="add_tiles",
    )(slots, tiles)


def split_kernel(orb_ref, out_ref, mark_ref):
    mark_ref[...] = jnp.zeros(mark_ref.shape, F32)

    def blocks(index):
        for b in index:
            high, rest = split(orb_ref[pl.ds(pl.multiple_of(b * TILE, TILE), TILE), :])
            out_ref[b, :TILE] = high
            out_ref[b, TILE:] = rest

    in_groups(out_ref.shape[0], blocks, 2)


def split_orbitals(orbitals, parts):
    count, nocc = orbitals.shape
    return pl.pallas_call(
        split_kernel,
        out_shape=(
            jax.ShapeDtypeStruct((count // TILE, 2 * TILE, nocc), BF16),
            jax.ShapeDtypeStruct((8, LANES), F32),
        ),
        grid=(parts,),
        in_specs=[pl.BlockSpec((count // parts, nocc), lambda g: (g, 0))],
        out_specs=(
            pl.BlockSpec((count // parts // TILE, 2 * TILE, nocc), lambda g: (g, 0, 0)),
            pl.BlockSpec((8, LANES), lambda g: (0, 0)),
        ),
        compiler_params=params(60),
        cost_estimate=pl.CostEstimate(
            flops=0, bytes_accessed=8 * count * nocc, transcendentals=0
        ),
        name="split_orbitals",
    )(orbitals)


def accumulate(read, count, orb, row_id, col_id, offset, sums):
    low = low_lanes((ROWS, LANES))
    nd = len(sums)

    def tiles(index):
        products = []
        for s in index:
            left = []
            for d in range(nd):
                tile = read(d, s)
                turned = pltpu.roll(tile, TILE, 1)
                left += [split(jnp.where(low, tile, turned)), split(jnp.where(low, turned, tile))]
            pair = orb[col_id[offset + s]]
            if nd > 1:
                left = jnp.concatenate([jnp.concatenate(parts, axis=1) for parts in left], axis=0)
                products.append(dot(left, jnp.concatenate([pair, pair], axis=0)))
            else:
                left = jnp.concatenate([parts[k] for k in range(2) for parts in left], axis=0)
                product = dot(left, pair)
                products.append(product[:TILE] + product[TILE:])
        for s, product in zip(index, products):
            block = row_id[offset + s]
            for d in range(nd):
                sums[d][block] += product[d * TILE : (d + 1) * TILE]

    in_groups(count, tiles, 16 if nd > 1 else 32)


def whole(a):
    return pl.BlockSpec(a.shape, lambda g, *_, n=len(a.shape): (0,) * n)


def orb_spec(blocks, orbs, which):
    return pl.BlockSpec((blocks,) + orbs.shape[1:], lambda g, *t: (which(*t), 0, 0))


def call(kernel, name, tables, args, specs, out, scratch, products, mib=60):
    single = not isinstance(out, (tuple, list))
    return pl.pallas_call(
        kernel,
        out_shape=out,
        grid_spec=pltpu.PrefetchScalarGridSpec(
            num_scalar_prefetch=len(tables),
            grid=(1,),
            in_specs=specs,
            out_specs=whole(out) if single else [whole(o) for o in out],
            scratch_shapes=scratch,
        ),
        compiler_params=params(mib),
        cost_estimate=pl.CostEstimate(
            flops=products * 100_000_000, bytes_accessed=2**23, transcendentals=0
        ),
        name=name,
    )(*tables, *args)


def rows_kernel(count, nd, fresh, row_id, col_id, place_ref, *refs):
    chunks = [refs[2 * k : 2 * k + 2] for k in range(count)]
    orbs, refs = refs[2 * count : 3 * count], refs[3 * count :]
    if fresh:
        sums = refs
        for total in sums:
            total[...] = jnp.zeros(total.shape, F32)
    else:
        before, sums, sem = refs[:nd], refs[nd : 2 * nd], refs[2 * nd]
        loads = [pltpu.make_async_copy(before[d], sums[d], sem.at[d]) for d in range(nd)]
        for load in loads:
            load.start()
        for load in loads:
            load.wait()
    offset = 0
    for (head, rest), orb in zip(chunks, orbs):
        read = lambda d, s, head=head, rest=rest: head[d, s] if d < nd - 1 else rest[0, s]
        accumulate(read, head.shape[1], orb, row_id, col_id, offset, sums)
        offset += head.shape[1]


def add_rows(totals, chunks, where, orbs, row_blocks, col_blocks):
    count = len(chunks)
    nd, slots = chunks[0][0].shape[0] + 1, chunks[0][0].shape[1]
    args = [part for chunk in chunks for part in chunk]
    specs = [whole(c) for c in args]
    specs += [orb_spec(col_blocks, orbs, lambda r, c, p, k=k: p[k]) for k in range(count)]
    args += [orbs] * count
    scratch = []
    if totals is not None:
        specs += [pl.BlockSpec(memory_space=pl.ANY)] * nd
        args += totals
        scratch.append(pltpu.SemaphoreType.DMA((nd,)))
    out = jax.ShapeDtypeStruct((row_blocks, TILE, orbs.shape[2]), F32)
    return call(
        functools.partial(rows_kernel, count, nd, totals is None), "add_rows", where, args, specs,
        [out] * nd, scratch, count * slots,
    )


def piece_kernel(count, halves, at, row_id, col_id, place_ref, *refs):
    chunks, refs = refs[:count], refs[count:]
    orbs_ref, in_ref, diag_ref, energy_ref, piece_ref, total_ref, sums, square, chunk_buf, orb_buf = refs[:10]
    sem, chunk_sem, orb_sem = refs[10:]
    ranges = count - halves
    col_blocks = orb_buf.shape[1]
    load = pltpu.make_async_copy(in_ref, sums, sem)
    load.start()
    moves = []
    for k in range(count):
        size = chunks[k].shape[1]
        start = chunks[0].shape[1] if halves and k == count - 1 else 0
        start = start // 2
        target = chunk_buf.at[min(k, ranges - 1), pl.ds(start, size)]
        source = chunks[k].at[min(at, chunks[k].shape[0] - 1)]
        moves.append(pltpu.make_async_copy(source, target, chunk_sem.at[k]))
        moves[-1].start()
        if k < ranges:
            source = orbs_ref.at[pl.ds(place_ref[k] * col_blocks, col_blocks)]
            moves.append(pltpu.make_async_copy(source, orb_buf.at[k], orb_sem.at[k]))
            moves[-1].start()
    load.wait()
    offset = 0
    for k in range(ranges):
        for move in moves[2 * k : 2 * k + 2 + (halves if k == ranges - 1 else 0)]:
            move.wait()
        read = lambda d, s, k=k: chunk_buf[k, s]
        accumulate(read, chunk_buf.shape[1], orb_buf.at[k], row_id, col_id, offset, [sums])
        offset += chunk_buf.shape[1]
    store = pltpu.make_async_copy(sums, total_ref, sem)
    store.start()
    first = place_ref[ranges] * piece_ref.shape[0]
    energy = energy_ref[...]

    def blocks(index):
        for b in index:
            value = sums[first + b] * (-1.0 / (diag_ref[first + b] - energy))
            for k in range(square.shape[1]):
                lanes = slice(k * LANES, (k + 1) * LANES)
                for parity in range(2):
                    square[b % 4, k, pl.ds(parity, ROWS, stride=2), :] = value[
                        parity * ROWS : (parity + 1) * ROWS, lanes
                    ]
                piece_ref[b, :, lanes] = square[b % 4, k]

    in_groups(piece_ref.shape[0], blocks, 4)
    store.wait()


def response_piece(total, chunks, at, where, orbs, diag, energy, col_blocks):
    count = len(chunks)
    halves = int(chunks[-1].shape[1] != chunks[0].shape[1])
    ranges = count - halves
    nocc = orbs.shape[2]
    hbm = pl.BlockSpec(memory_space=pl.ANY)
    piece = jax.ShapeDtypeStruct((col_blocks, TILE, nocc), F32)
    return pl.pallas_call(
        functools.partial(piece_kernel, count, halves, at),
        out_shape=(piece, jax.ShapeDtypeStruct(total.shape, F32)),
        grid_spec=pltpu.PrefetchScalarGridSpec(
            num_scalar_prefetch=3,
            grid=(1,),
            in_specs=[hbm] * (count + 2) + [whole(diag), whole(energy)],
            out_specs=(whole(piece), hbm),
            scratch_shapes=[
                pltpu.VMEM(total.shape, F32),
                pltpu.VMEM((4, nocc // LANES, TILE, LANES), F32),
                pltpu.VMEM((ranges,) + chunks[0].shape[1:], F32),
                pltpu.VMEM((ranges, col_blocks) + orbs.shape[1:], BF16),
                pltpu.SemaphoreType.DMA,
                pltpu.SemaphoreType.DMA((count,)),
                pltpu.SemaphoreType.DMA((ranges,)),
            ],
        ),
        compiler_params=params(60),
        cost_estimate=pl.CostEstimate(
            flops=20_000_000_000, bytes_accessed=2**23, transcendentals=0
        ),
        name="response_piece",
    )(*where, *chunks, orbs, total, diag, energy)


def first_tiles(totals, diag_ref, energy_ref, orb_ref, row_id, col_id, out_ref):
    low = low_lanes((ROWS, LANES))

    def tiles(index):
        for s in index:
            block = row_id[s]
            inverse = -1.0 / (diag_ref[block] - energy_ref[...])
            left = [part for total in totals for part in split(total[block] * inverse)]
            value = dot_nt(jnp.concatenate(left, axis=0), orb_ref[col_id[s]])
            for d in range(len(totals)):
                start = 2 * d * TILE
                tile = value[start : start + TILE] + value[start + TILE : start + 2 * TILE]
                tile = tile + pltpu.roll(tile, TILE, 1)
                rows = pl.ds(pl.multiple_of(s * ROWS, ROWS), ROWS)
                out_ref[d, rows, :] = jnp.where(low, tile[:ROWS], tile[ROWS:])

    in_groups(out_ref.shape[1] // ROWS, tiles, 8)


def second_tiles(x_ref, orb_ref, row_id, col_id, square, read, write):
    low = low_lanes((ROWS, LANES))
    count = x_ref.shape[0]

    def tiles(index):
        for u, s in enumerate(index):
            right = [part for d in range(count) for part in split(x_ref[d, col_id[s]])]
            value = dot_nt(orb_ref[row_id[s]], jnp.concatenate(right, axis=0))
            value = value[:TILE] + value[TILE:]
            for d in range(count):
                tile = value[:, d * LANES : (d + 1) * LANES]
                square[d, u] = tile + pltpu.roll(tile, TILE, 1)
        for u, s in enumerate(index):
            rows = pl.ds(pl.multiple_of(s * ROWS, ROWS), ROWS)
            for d in range(count):
                even = square[d, u, pl.ds(0, ROWS, stride=2), :]
                odd = square[d, u, pl.ds(1, ROWS, stride=2), :]
                write(d, rows, read(d, rows) + jnp.where(low, even, odd))

    in_groups(row_id.shape[0], tiles, square.shape[1])


def fetch(place_ref, ways, x_ref, sem):
    for k, way in enumerate(ways):

        @pl.when(place_ref[1] == k)
        def _(way=way):
            pltpu.make_async_copy(way, x_ref, sem).start()

    return pltpu.make_async_copy(ways[0], x_ref, sem).wait


def early_kernel(nd, way_count, row_id, col_id, place_ref, *refs):
    ways = [refs[d * way_count : (d + 1) * way_count] for d in range(nd - 1)]
    refs = refs[(nd - 1) * way_count :]
    totals, refs = refs[:nd], refs[nd:]
    diag_ref, energy_ref, orb_cols, orb_rows, out_ref, x_ref, square, sem = refs
    waits = [fetch(place_ref, ways[d], x_ref.at[d], sem.at[d]) for d in range(nd - 1)]
    first_tiles(totals, diag_ref, energy_ref, orb_cols, row_id, col_id, out_ref)
    for wait in waits:
        wait()

    def write(d, rows, value):
        out_ref[d, rows, :] = value

    second_tiles(
        x_ref, orb_rows, row_id, col_id, square, lambda d, rows: out_ref[d, rows, :], write
    )


def early_terms(own, places, ways, totals, diag, energy, orbs, row_blocks, col_blocks):
    nd, slots = len(totals), own[0].shape[0]
    shape = ways[0][0].shape
    flat = [way for each in ways for way in each]
    specs = [pl.BlockSpec(memory_space=pl.ANY)] * len(flat)
    specs += [whole(a) for a in [*totals, diag, energy]]
    specs.append(orb_spec(col_blocks, orbs, lambda r, c, p: p[2]))
    specs.append(orb_spec(row_blocks, orbs, lambda r, c, p: p[0]))
    return call(
        functools.partial(early_kernel, nd, len(ways[0])), "early_terms", [*own, places],
        [*flat, *totals, diag, energy, orbs, orbs], specs,
        jax.ShapeDtypeStruct((nd, slots * ROWS, LANES), F32),
        [
            pltpu.VMEM((nd - 1,) + shape, F32),
            pltpu.VMEM((nd - 1, 8, TILE, LANES), F32),
            pltpu.SemaphoreType.DMA((nd - 1,)),
        ],
        1,
    )


def last_kernel(way_count, row_id, col_id, place_ref, *refs):
    ways, refs = refs[:way_count], refs[way_count:]
    orb_rows, done_ref, out_ref, x_ref, square, rows_ref, sem = refs
    wait = fetch(place_ref, ways, x_ref.at[0], sem)
    nd, slots, area = out_ref.shape

    def layout(d, source):
        for start in range(0, slots, 8):
            for k in range(area // LANES):
                out_ref[d, start : start + 8, k * LANES : (k + 1) * LANES] = source[
                    pl.ds(start * ROWS + k, 8, stride=ROWS), :
                ]

    for d in range(nd - 1):
        layout(d, done_ref.at[d])
    wait()

    def write(d, rows, value):
        rows_ref[rows, :] = value

    second_tiles(
        x_ref, orb_rows, row_id, col_id, square, lambda d, rows: done_ref[nd - 1, rows, :], write
    )
    layout(nd - 1, rows_ref)


def last_terms(own, places, ways, done, orbs, row_blocks):
    slots = own[0].shape[0]
    nd = done.shape[0]
    specs = [pl.BlockSpec(memory_space=pl.ANY)] * len(ways)
    specs += [orb_spec(row_blocks, orbs, lambda r, c, p: p[0]), whole(done)]
    return call(
        functools.partial(last_kernel, len(ways)), "last_terms", [*own, places],
        [*ways, orbs, done], specs,
        jax.ShapeDtypeStruct((nd, slots, ROWS * LANES), F32),
        [
            pltpu.VMEM((1,) + ways[0].shape, F32),
            pltpu.VMEM((1, 8, TILE, LANES), F32),
            pltpu.VMEM((slots * ROWS, LANES), F32),
            pltpu.SemaphoreType.DMA,
        ],
        slots,
        mib=32,
    )


def tie(values, others=()):
    hbm = pl.BlockSpec(memory_space=pl.ANY)
    count = len(values)
    return pl.pallas_call(
        lambda *refs: None,
        out_shape=[jax.ShapeDtypeStruct(v.shape, v.dtype) for v in values],
        in_specs=[hbm] * (count + len(others)),
        out_specs=[hbm] * count,
        input_output_aliases={k: k for k in range(count)},
        name="tie",
    )(*values, *others)


def ring_order(count):
    return list(range(0, count, 2)) + list(range(count - 1, 0, -2))


def row_broadcast(value, row_count, col_count, ratio, held=None):
    def send(k):
        parent = k & (k - 1)
        if k & 1:
            rows = [[(r, r ^ 1) for r in range(row_count)]] * col_count
        else:
            rows = [[(c // ratio ^ parent, c // ratio ^ k)] for c in range(col_count)]
        pairs = [(a * col_count + c, b * col_count + c) for c in range(col_count) for a, b in rows[c]]
        return lax.ppermute(ways[parent], ("row", "col"), pairs)

    ways = [value] + [None] * (row_count - 1)
    for k in range(2, row_count, 2):
        ways[k] = send(k)
    if held is not None:
        mark = held()
        for k in range(2, row_count, 2):
            ways[k] = tie([ways[k]], [mark])[0]
    for k in range(1, row_count, 2):
        ways[k] = send(k)
    return ways


def local(
    density_tiles,
    tile_ids,
    batch_blocks,
    basis_values,
    grid_weight,
    xc_kernel,
    grid_coord,
    orbitals,
    precond_diag,
    orbital_energy,
):
    row_count = lax.axis_size("row")
    col_count = lax.axis_size("col")
    device_count = row_count * col_count
    own_row = lax.axis_index("row")
    own_col = lax.axis_index("col")
    own_index = own_row * col_count + own_col
    block_count = NB // TILE
    row_blocks = block_count // row_count
    col_blocks = block_count // col_count
    per_range = FB // row_count
    slot_count = tile_ids.shape[0]
    ratio = col_count // row_count
    col_width = col_blocks * TILE
    nd = density_tiles.shape[0]
    nocc = orbitals.shape[1]

    ask = batch_blocks
    match = ask // col_blocks == own_col
    ask_col = jnp.sum(jnp.where(match, ask, 0), axis=1)
    ask_row = lax.dynamic_slice_in_dim(ask, own_row * per_range, per_range, 1)
    wanted = jnp.where(jnp.any(match, axis=1)[:, None], ask_row * block_count + ask_col[:, None], -1)
    hit = wanted.reshape(-1)[:, None] == tile_ids[None, :]
    slots = jnp.max(jnp.where(hit, jnp.arange(slot_count, dtype=jnp.int32)[None, :], -1), axis=1)
    own_cols = lax.dynamic_slice_in_dim(ask, own_index, 1, 0)[0] // col_blocks

    local_rows = tile_ids // block_count - own_row * row_blocks
    local_cols = tile_ids % col_blocks

    order = ring_order(col_count)
    place = [order.index(c) for c in range(col_count)]
    forward = [(order[i], order[(i + 1) % col_count]) for i in range(col_count)]
    backward = [(b, a) for a, b in forward]
    ring = jnp.asarray(order, jnp.int32)
    at = jnp.asarray(place, jnp.int32)[own_col]
    part = own_col % ratio
    half = slot_count // 2
    steps = col_count // 2 - 1

    diag = precond_diag.reshape(row_blocks, ROWS, 2).swapaxes(1, 2).reshape(row_blocks, TILE, 1)
    term_place = jnp.stack([own_row, own_row ^ (own_col // ratio), own_col])

    all_orbitals = lax.all_gather(orbitals, "row", axis=0, tiled=True)
    pad = -slot_count % (8 * LANES)
    ids = jnp.pad(tile_ids, (0, pad)).reshape(-1, LANES).astype(F32)
    picked = pick_tiles(slots, density_tiles, ids, device_count)
    exchange = lambda a: lax.all_to_all(
        a, ("row", "col"), split_axis=0, concat_axis=0, tiled=True
    )
    arrived = exchange(picked)
    listed = lax.dynamic_slice(
        arrived, (own_row * col_count, arrived.shape[1] - ids.shape[0], 0), (col_count,) + ids.shape
    )
    listed = listed.reshape(col_count, -1)[:, :slot_count].astype(jnp.int32)
    listed_rows = listed // block_count - own_row * row_blocks
    listed_cols = listed % col_blocks

    def plan(offsets):
        cols = ring[(at + jnp.asarray(offsets, jnp.int32)) % col_count]
        rows = listed_rows[cols].reshape(-1)
        blocks = listed_cols[cols].reshape(-1)
        return rows, blocks, jnp.append(cols, part)

    plans = [plan((0, -1, 1))]
    plans += [plan((-step, step)) for step in range(2, steps)]
    plans[-1:] = [plan((-steps + 1, steps - 1, -steps, steps, col_count // 2))]
    tables = (diag, local_rows, local_cols, term_place)
    arrived, tables = lax.optimization_barrier((arrived, tables))
    diag, local_rows, local_cols, term_place = tables
    built = batch_tiles(
        per_range, col_count, own_cols, arrived, basis_values[0], grid_weight, xc_kernel, grid_coord
    )
    returned = exchange(built)
    hams = add_tiles(slots, returned, slot_count, nd)

    orbs, mark = split_orbitals(all_orbitals, col_count)

    own = (local_rows, local_cols)
    energy = orbital_energy[None]
    send_up = lambda a: lax.ppermute(a, "col", forward)
    send_down = lambda a: lax.ppermute(a, "col", backward)

    marks = [mark, diag, *(table for where in plans for table in where)]
    held = tie([send_up(a) for a in hams] + [send_down(a) for a in hams], marks)
    ups, downs = list(held[:2]), list(held[2:])
    totals = None
    for step in range(2, steps):
        chunks = [hams, ups, downs] if totals is None else [ups, downs]
        sums = add_rows(totals, chunks, plans[step - 2], orbs, row_blocks, col_blocks)
        up, down = send_up(ups[0]), send_down(downs[0])
        if step < steps - 1:
            ups[1], downs[1] = send_up(ups[1]), send_down(downs[1])
        ups[0], downs[0], ups[1], downs[1], *totals = tie([up, down, ups[1], downs[1], *sums])

    def opposite(up, down):
        return [send_up(up[:, :half]), send_down(down[:, half:])]

    def finish(d, chunks):
        return response_piece(
            totals[d], chunks, d % (nd - 1), plans[-1], orbs, diag, energy, col_blocks
        )

    def spread(piece, held=None):
        return row_broadcast(piece, row_count, col_count, ratio, held)

    up3, down3, *totals = tie([send_up(ups[0]), send_down(downs[0]), *totals])
    pieces, sums, ways = [], [], []
    held = tie([*opposite(up3[:1], down3[:1]), up3, down3, ups[1], downs[1], *totals])
    for d in range(nd - 1):
        up_end, down_end, up3, down3, ups[1], downs[1], *totals[d:] = held
        later = [up_end, down_end]
        if d < nd - 2:
            later = opposite(up3[d + 1 : d + 2], down3[d + 1 : d + 2])
        if d == 0:
            last2 = [send_up(ups[1]), send_down(downs[1])]
        if d == nd - 2:
            last3 = [send_up(last2[0]), send_down(last2[1])]
        piece, total = finish(d, [ups[0], downs[0], up3, down3, up_end, down_end])
        pieces.append(piece)
        sums.append(total)
        ways.append(spread(piece) if d == 0 else None)
        if d < nd - 2:
            held = tie([*later, up3, down3, *last2, *totals[d + 1 :]], [total])
            last2 = held[4:6]
    last2 = list(last2)
    last3[0], last3[1], last2[0], last2[1], totals[-1] = tie([*last3, *last2, totals[-1]], [sums[-1]])
    up_end, down_end, *last3, last2[0], last2[1], totals[-1] = tie(
        [*opposite(*last3), *last3, *last2, totals[-1]], [ways[0][row_count // 2]]
    )
    piece, total = finish(nd - 1, [*last2, *last3, up_end, down_end])
    sums.append(total)
    ways = ways[:1]
    for d in range(1, nd - 1):
        ways.append(spread(pieces[d], lambda: sums[-1]))
    piece = tie([piece], [way[row_count // 2] for way in ways])[0]
    done = early_terms(own, term_place, ways, sums, diag, energy, orbs, row_blocks, col_blocks)
    ways.append(spread(piece, lambda: done))
    return last_terms(own, term_place, ways[-1], done, orbs, row_blocks)


def solution(mesh):
    placed = (
        P(None, ("row", "col"), None),
        P(("row", "col")),
        P(),
        P(("row", "col"), None, None),
        P(("row", "col"), None),
        P(("row", "col"), None),
        P(None, ("row", "col"), None),
        P("row", None),
        P("row"),
        P(),
    )
    return jax.shard_map(
        local, mesh=mesh, in_specs=placed, out_specs=P(None, ("row", "col"), None), check_vma=False
    )
```

```python
import functools

import jax
import jax.numpy as jnp
from jax import lax
from jax.experimental import pallas as pl
from jax.experimental.pallas import tpu as pltpu
from jax.sharding import PartitionSpec as P

NB = 8192
TILE = 64
FB = 8
LANES = 2 * TILE
ROWS = TILE * TILE // LANES
F32 = jnp.float32
BF16 = jnp.bfloat16
NT = (((1,), (1,)), ((), ()))


def split(value):
    high = value.astype(BF16)
    return high, (value - high.astype(F32)).astype(BF16)


def dot(a, b):
    return jnp.dot(a, b, preferred_element_type=F32)


def dot_nt(a, b):
    return lax.dot_general(a, b, NT, preferred_element_type=F32)


def low_lanes(shape):
    return lax.broadcasted_iota(jnp.int32, shape, len(shape) - 1) < TILE


def params(mib):
    return pltpu.CompilerParams(vmem_limit_bytes=mib * 2**20)


VMEM = pl.BlockSpec(memory_space=pltpu.VMEM)
SMEM = pl.BlockSpec(memory_space=pltpu.SMEM)


def in_groups(count, body, group=16):
    if count % group:
        group = 1

    def step(g, carry):
        body([g * group + u for u in range(group)])
        return carry

    lax.fori_loop(0, count // group, step, 0)


def pick_kernel(slot_ref, tiles_ref, ids_ref, out_ref, rows):
    nd, slots, area = tiles_ref.shape
    per_range = slot_ref.shape[0] // out_ref.shape[0]
    for d in range(nd):
        for start in range(0, slots, 8):
            for k in range(area // LANES):
                rows[d, pl.ds(start * ROWS + k, 8, stride=ROWS), :] = tiles_ref[
                    d, start : start + 8, k * LANES : (k + 1) * LANES
                ]

    def device(index):
        for n in index:
            for k in range(per_range):
                slot = slot_ref[n * per_range + k]
                first = pl.multiple_of(jnp.maximum(slot, 0) * ROWS, ROWS)
                for d in range(nd):
                    out_ref[n, (k * nd + d) * ROWS : (k * nd + d + 1) * ROWS] = jnp.where(
                        slot >= 0, rows[d, pl.ds(first, ROWS), :], 0.0
                    )
            out_ref[n, per_range * nd * ROWS :] = ids_ref[...]

    in_groups(out_ref.shape[0], device, 2)


def pick_tiles(slots, tiles, ids, device_count):
    nd, count, area = tiles.shape
    rows = slots.shape[0] // device_count * nd * ROWS + ids.shape[0]
    return pl.pallas_call(
        pick_kernel,
        out_shape=jax.ShapeDtypeStruct((device_count, rows, LANES), F32),
        in_specs=[SMEM, VMEM, VMEM],
        out_specs=VMEM,
        scratch_shapes=[pltpu.VMEM((nd, count * ROWS, LANES), F32)],
        compiler_params=params(32),
        name="pick_tiles",
    )(slots, tiles, ids)


def batch_kernel(
    per_range, col_count, col_ref, tiles_ref, basis_ref, weight_ref, xc_ref, coord_ref, out_ref,
    bh, bl, wh, wl, square,
):
    nd = coord_ref.shape[0]
    width, pts = basis_ref.shape
    low = low_lanes((ROWS, LANES))
    if col_count > FB:
        out_ref[...] = jnp.zeros(out_ref.shape, F32)

    def place(i, j, d):
        owner = (i // per_range) * col_count + col_ref[j]
        return owner, pl.ds(pl.multiple_of((i % per_range * nd + d) * ROWS, ROWS), ROWS)

    high, rest = split(basis_ref[...])
    bh[...] = high
    bl[...] = rest

    def direction(d, carry):
        for i in range(FB):
            for jj in range(FB // 2):
                first = tiles_ref[place(i, 2 * jj, d)]
                second = tiles_ref[place(i, 2 * jj + 1, d)]
                square[jj, pl.ds(i * TILE, ROWS, stride=2), :] = jnp.where(
                    low, first, pltpu.roll(second, TILE, 1)
                )
                square[jj, pl.ds(i * TILE + 1, ROWS, stride=2), :] = jnp.where(
                    low, pltpu.roll(first, TILE, 1), second
                )
        eh, el = split(jnp.concatenate([square[jj] for jj in range(FB // 2)], axis=1))
        piece = 256
        for start in range(0, pts, piece):
            cols = slice(start, start + piece)
            projected = dot(eh, bh[:, cols]) + dot(eh, bl[:, cols]) + dot(el, bh[:, cols])
            values = basis_ref[:, cols]
            response = jnp.sum(values * projected, axis=0, keepdims=True)
            potential = xc_ref[:, cols] * response + coord_ref[d, :, cols]
            weighted = values * (weight_ref[:, cols] * potential)
            high, rest = split(weighted)
            wh[:, cols] = high
            wl[:, cols] = rest
        for start in range(0, width, piece):
            rows = slice(start, start + piece)
            value = (
                dot_nt(wh[...], bh[rows]) + dot_nt(wh[...], bl[rows]) + dot_nt(wl[...], bh[rows])
            )
            for lane in range(0, piece, LANES):
                square[(start + lane) // LANES] = value[:, lane : lane + LANES]
        for i in range(FB):
            for jj in range(FB // 2):
                even = square[jj, pl.ds(i * TILE, ROWS, stride=2), :]
                odd = square[jj, pl.ds(i * TILE + 1, ROWS, stride=2), :]
                out_ref[place(i, 2 * jj, d)] = jnp.where(low, even, pltpu.roll(odd, TILE, 1))
                out_ref[place(i, 2 * jj + 1, d)] = jnp.where(low, pltpu.roll(even, TILE, 1), odd)
        return carry

    lax.fori_loop(0, nd, direction, 0)


def batch_tiles(per_range, col_count, cols, tiles, basis, weight, xc, coord):
    width, pts = basis.shape
    return pl.pallas_call(
        functools.partial(batch_kernel, per_range, col_count),
        out_shape=jax.ShapeDtypeStruct(
            (tiles.shape[0], per_range * coord.shape[0] * ROWS, LANES), F32
        ),
        in_specs=[SMEM] + [VMEM] * 5,
        out_specs=VMEM,
        scratch_shapes=[
            pltpu.VMEM((width, pts), BF16),
            pltpu.VMEM((width, pts), BF16),
            pltpu.VMEM((width, pts), BF16),
            pltpu.VMEM((width, pts), BF16),
            pltpu.VMEM((width // LANES, width, LANES), F32),
        ],
        compiler_params=params(48),
        name="batch_tiles",
    )(cols, tiles, basis, weight, xc, coord)


def add_kernel(slot_ref, tiles_ref, head_ref, rest_ref):
    nd = head_ref.shape[0] + 1
    per_range = slot_ref.shape[0] // tiles_ref.shape[0]
    head_ref[...] = jnp.zeros(head_ref.shape, F32)
    rest_ref[...] = jnp.zeros(rest_ref.shape, F32)

    def step(n, carry):
        for k in range(per_range):
            slot = slot_ref[n * per_range + k]

            @pl.when(slot >= 0)
            def _(slot=slot, k=k):
                for d in range(nd):
                    start = (k * nd + d) * ROWS
                    ref, at = (head_ref, d) if d < nd - 1 else (rest_ref, 0)
                    ref[at, slot] += tiles_ref[n, start : start + ROWS]

        return carry

    lax.fori_loop(0, tiles_ref.shape[0], step, 0)


def add_tiles(slots, tiles, slot_count, nd):
    return pl.pallas_call(
        add_kernel,
        out_shape=[jax.ShapeDtypeStruct((n, slot_count, ROWS, LANES), F32) for n in (nd - 1, 1)],
        in_specs=[SMEM, VMEM],
        out_specs=[VMEM, VMEM],
        compiler_params=params(32),
        name="add_tiles",
    )(slots, tiles)


def split_kernel(orb_ref, out_ref, mark_ref):
    mark_ref[...] = jnp.zeros(mark_ref.shape, F32)

    def blocks(index):
        for b in index:
            high, rest = split(orb_ref[pl.ds(pl.multiple_of(b * TILE, TILE), TILE), :])
            out_ref[b, :TILE] = high
            out_ref[b, TILE:] = rest

    in_groups(out_ref.shape[0], blocks, 2)


def split_orbitals(orbitals, parts):
    count, nocc = orbitals.shape
    return pl.pallas_call(
        split_kernel,
        out_shape=(
            jax.ShapeDtypeStruct((count // TILE, 2 * TILE, nocc), BF16),
            jax.ShapeDtypeStruct((8, LANES), F32),
        ),
        grid=(parts,),
        in_specs=[pl.BlockSpec((count // parts, nocc), lambda g: (g, 0))],
        out_specs=(
            pl.BlockSpec((count // parts // TILE, 2 * TILE, nocc), lambda g: (g, 0, 0)),
            pl.BlockSpec((8, LANES), lambda g: (0, 0)),
        ),
        compiler_params=params(60),
        cost_estimate=pl.CostEstimate(
            flops=0, bytes_accessed=8 * count * nocc, transcendentals=0
        ),
        name="split_orbitals",
    )(orbitals)


def accumulate(read, count, orb, row_id, col_id, offset, sums):
    low = low_lanes((ROWS, LANES))
    nd = len(sums)

    def tiles(index):
        products = []
        for s in index:
            left = []
            for d in range(nd):
                tile = read(d, s)
                turned = pltpu.roll(tile, TILE, 1)
                left += [split(jnp.where(low, tile, turned)), split(jnp.where(low, turned, tile))]
            pair = orb[col_id[offset + s]]
            if nd > 1:
                left = jnp.concatenate([jnp.concatenate(parts, axis=1) for parts in left], axis=0)
                products.append(dot(left, jnp.concatenate([pair, pair], axis=0)))
            else:
                left = jnp.concatenate([parts[k] for k in range(2) for parts in left], axis=0)
                product = dot(left, pair)
                products.append(product[:TILE] + product[TILE:])
        for s, product in zip(index, products):
            block = row_id[offset + s]
            for d in range(nd):
                sums[d][block] += product[d * TILE : (d + 1) * TILE]

    in_groups(count, tiles, 16 if nd > 1 else 32)


def whole(a):
    return pl.BlockSpec(a.shape, lambda g, *_, n=len(a.shape): (0,) * n)


def orb_spec(blocks, orbs, which):
    return pl.BlockSpec((blocks,) + orbs.shape[1:], lambda g, *t: (which(*t), 0, 0))


def call(kernel, name, tables, args, specs, out, scratch, products, mib=60):
    single = not isinstance(out, (tuple, list))
    return pl.pallas_call(
        kernel,
        out_shape=out,
        grid_spec=pltpu.PrefetchScalarGridSpec(
            num_scalar_prefetch=len(tables),
            grid=(1,),
            in_specs=specs,
            out_specs=whole(out) if single else [whole(o) for o in out],
            scratch_shapes=scratch,
        ),
        compiler_params=params(mib),
        cost_estimate=pl.CostEstimate(
            flops=products * 100_000_000, bytes_accessed=2**23, transcendentals=0
        ),
        name=name,
    )(*tables, *args)


def rows_kernel(count, nd, fresh, row_id, col_id, place_ref, *refs):
    chunks = [refs[2 * k : 2 * k + 2] for k in range(count)]
    orbs, refs = refs[2 * count : 3 * count], refs[3 * count :]
    if fresh:
        sums = refs
        for total in sums:
            total[...] = jnp.zeros(total.shape, F32)
    else:
        before, sums, sem = refs[:nd], refs[nd : 2 * nd], refs[2 * nd]
        loads = [pltpu.make_async_copy(before[d], sums[d], sem.at[d]) for d in range(nd)]
        for load in loads:
            load.start()
        for load in loads:
            load.wait()
    offset = 0
    for (head, rest), orb in zip(chunks, orbs):
        read = lambda d, s, head=head, rest=rest: head[d, s] if d < nd - 1 else rest[0, s]
        accumulate(read, head.shape[1], orb, row_id, col_id, offset, sums)
        offset += head.shape[1]


def add_rows(totals, chunks, where, orbs, row_blocks, col_blocks):
    count = len(chunks)
    nd, slots = chunks[0][0].shape[0] + 1, chunks[0][0].shape[1]
    args = [part for chunk in chunks for part in chunk]
    specs = [whole(c) for c in args]
    specs += [orb_spec(col_blocks, orbs, lambda r, c, p, k=k: p[k]) for k in range(count)]
    args += [orbs] * count
    scratch = []
    if totals is not None:
        specs += [pl.BlockSpec(memory_space=pl.ANY)] * nd
        args += totals
        scratch.append(pltpu.SemaphoreType.DMA((nd,)))
    out = jax.ShapeDtypeStruct((row_blocks, TILE, orbs.shape[2]), F32)
    return call(
        functools.partial(rows_kernel, count, nd, totals is None), "add_rows", where, args, specs,
        [out] * nd, scratch, count * slots,
    )


def piece_kernel(count, halves, at, row_id, col_id, place_ref, *refs):
    chunks, refs = refs[:count], refs[count:]
    orbs_ref, in_ref, diag_ref, energy_ref, piece_ref, total_ref, sums, square, chunk_buf, orb_buf = refs[:10]
    sem, chunk_sem, orb_sem = refs[10:]
    ranges = count - halves
    col_blocks = orb_buf.shape[1]
    load = pltpu.make_async_copy(in_ref, sums, sem)
    load.start()
    moves = []
    for k in range(count):
        size = chunks[k].shape[1]
        start = chunks[0].shape[1] if halves and k == count - 1 else 0
        start = start // 2
        target = chunk_buf.at[min(k, ranges - 1), pl.ds(start, size)]
        source = chunks[k].at[min(at, chunks[k].shape[0] - 1)]
        moves.append(pltpu.make_async_copy(source, target, chunk_sem.at[k]))
        moves[-1].start()
        if k < ranges:
            source = orbs_ref.at[pl.ds(place_ref[k] * col_blocks, col_blocks)]
            moves.append(pltpu.make_async_copy(source, orb_buf.at[k], orb_sem.at[k]))
            moves[-1].start()
    load.wait()
    offset = 0
    for k in range(ranges):
        for move in moves[2 * k : 2 * k + 2 + (halves if k == ranges - 1 else 0)]:
            move.wait()
        read = lambda d, s, k=k: chunk_buf[k, s]
        accumulate(read, chunk_buf.shape[1], orb_buf.at[k], row_id, col_id, offset, [sums])
        offset += chunk_buf.shape[1]
    store = pltpu.make_async_copy(sums, total_ref, sem)
    store.start()
    first = place_ref[ranges] * piece_ref.shape[0]
    energy = energy_ref[...]

    def blocks(index):
        for b in index:
            value = sums[first + b] * (-1.0 / (diag_ref[first + b] - energy))
            for k in range(square.shape[1]):
                lanes = slice(k * LANES, (k + 1) * LANES)
                for parity in range(2):
                    square[b % 4, k, pl.ds(parity, ROWS, stride=2), :] = value[
                        parity * ROWS : (parity + 1) * ROWS, lanes
                    ]
                piece_ref[b, :, lanes] = square[b % 4, k]

    in_groups(piece_ref.shape[0], blocks, 4)
    store.wait()


def response_piece(total, chunks, at, where, orbs, diag, energy, col_blocks):
    count = len(chunks)
    halves = int(chunks[-1].shape[1] != chunks[0].shape[1])
    ranges = count - halves
    nocc = orbs.shape[2]
    hbm = pl.BlockSpec(memory_space=pl.ANY)
    piece = jax.ShapeDtypeStruct((col_blocks, TILE, nocc), F32)
    return pl.pallas_call(
        functools.partial(piece_kernel, count, halves, at),
        out_shape=(piece, jax.ShapeDtypeStruct(total.shape, F32)),
        grid_spec=pltpu.PrefetchScalarGridSpec(
            num_scalar_prefetch=3,
            grid=(1,),
            in_specs=[hbm] * (count + 2) + [whole(diag), whole(energy)],
            out_specs=(whole(piece), hbm),
            scratch_shapes=[
                pltpu.VMEM(total.shape, F32),
                pltpu.VMEM((4, nocc // LANES, TILE, LANES), F32),
                pltpu.VMEM((ranges,) + chunks[0].shape[1:], F32),
                pltpu.VMEM((ranges, col_blocks) + orbs.shape[1:], BF16),
                pltpu.SemaphoreType.DMA,
                pltpu.SemaphoreType.DMA((count,)),
                pltpu.SemaphoreType.DMA((ranges,)),
            ],
        ),
        compiler_params=params(60),
        cost_estimate=pl.CostEstimate(
            flops=20_000_000_000, bytes_accessed=2**23, transcendentals=0
        ),
        name="response_piece",
    )(*where, *chunks, orbs, total, diag, energy)


def first_tiles(totals, diag_ref, energy_ref, orb_ref, row_id, col_id, out_ref):
    low = low_lanes((ROWS, LANES))

    def tiles(index):
        for s in index:
            block = row_id[s]
            inverse = -1.0 / (diag_ref[block] - energy_ref[...])
            left = [part for total in totals for part in split(total[block] * inverse)]
            value = dot_nt(jnp.concatenate(left, axis=0), orb_ref[col_id[s]])
            for d in range(len(totals)):
                start = 2 * d * TILE
                tile = value[start : start + TILE] + value[start + TILE : start + 2 * TILE]
                tile = tile + pltpu.roll(tile, TILE, 1)
                rows = pl.ds(pl.multiple_of(s * ROWS, ROWS), ROWS)
                out_ref[d, rows, :] = jnp.where(low, tile[:ROWS], tile[ROWS:])

    in_groups(out_ref.shape[1] // ROWS, tiles, 8)


def second_tiles(x_ref, orb_ref, row_id, col_id, square, read, write):
    low = low_lanes((ROWS, LANES))
    count = x_ref.shape[0]

    def tiles(index):
        for u, s in enumerate(index):
            right = [part for d in range(count) for part in split(x_ref[d, col_id[s]])]
            value = dot_nt(orb_ref[row_id[s]], jnp.concatenate(right, axis=0))
            value = value[:TILE] + value[TILE:]
            for d in range(count):
                tile = value[:, d * LANES : (d + 1) * LANES]
                square[d, u] = tile + pltpu.roll(tile, TILE, 1)
        for u, s in enumerate(index):
            rows = pl.ds(pl.multiple_of(s * ROWS, ROWS), ROWS)
            for d in range(count):
                even = square[d, u, pl.ds(0, ROWS, stride=2), :]
                odd = square[d, u, pl.ds(1, ROWS, stride=2), :]
                write(d, rows, read(d, rows) + jnp.where(low, even, odd))

    in_groups(row_id.shape[0], tiles, square.shape[1])


def fetch(place_ref, ways, x_ref, sem):
    for k, way in enumerate(ways):

        @pl.when(place_ref[1] == k)
        def _(way=way):
            pltpu.make_async_copy(way, x_ref, sem).start()

    return pltpu.make_async_copy(ways[0], x_ref, sem).wait


def early_kernel(nd, count, way_count, row_id, col_id, place_ref, *refs):
    ways = [refs[d * way_count : (d + 1) * way_count] for d in range(count)]
    refs = refs[count * way_count :]
    totals, refs = refs[:nd], refs[nd:]
    diag_ref, energy_ref, orb_cols, orb_rows, out_ref, x_ref, square, sem = refs
    waits = [fetch(place_ref, ways[d], x_ref.at[d], sem.at[d]) for d in range(count)]
    first_tiles(totals, diag_ref, energy_ref, orb_cols, row_id, col_id, out_ref)
    for wait in waits:
        wait()

    def write(d, rows, value):
        out_ref[d, rows, :] = value

    second_tiles(
        x_ref, orb_rows, row_id, col_id, square, lambda d, rows: out_ref[d, rows, :], write
    )


def early_terms(own, places, ways, totals, diag, energy, orbs, row_blocks, col_blocks):
    nd, slots = len(totals), own[0].shape[0]
    shape = ways[0][0].shape
    flat = [way for each in ways for way in each]
    specs = [pl.BlockSpec(memory_space=pl.ANY)] * len(flat)
    specs += [whole(a) for a in [*totals, diag, energy]]
    specs.append(orb_spec(col_blocks, orbs, lambda r, c, p: p[2]))
    specs.append(orb_spec(row_blocks, orbs, lambda r, c, p: p[0]))
    return call(
        functools.partial(early_kernel, nd, len(ways), len(ways[0])), "early_terms", [*own, places],
        [*flat, *totals, diag, energy, orbs, orbs], specs,
        jax.ShapeDtypeStruct((nd, slots * ROWS, LANES), F32),
        [
            pltpu.VMEM((len(ways),) + shape, F32),
            pltpu.VMEM((len(ways), 8, TILE, LANES), F32),
            pltpu.SemaphoreType.DMA((len(ways),)),
        ],
        1,
    )


def last_kernel(count, way_count, row_id, col_id, place_ref, *refs):
    ways = [refs[d * way_count : (d + 1) * way_count] for d in range(count)]
    refs = refs[count * way_count :]
    orb_rows, done_ref, out_ref, x_ref, square, rows_ref, sem = refs
    waits = [fetch(place_ref, ways[d], x_ref.at[d], sem.at[d]) for d in range(count)]
    nd, slots, area = out_ref.shape
    early = nd - count

    def layout(d, source):
        for start in range(0, slots, 8):
            for k in range(area // LANES):
                out_ref[d, start : start + 8, k * LANES : (k + 1) * LANES] = source[
                    pl.ds(start * ROWS + k, 8, stride=ROWS), :
                ]

    for d in range(early):
        layout(d, done_ref.at[d])
    for wait in waits:
        wait()

    def write(d, rows, value):
        rows_ref[d, rows, :] = value

    second_tiles(
        x_ref, orb_rows, row_id, col_id, square, lambda d, rows: done_ref[early + d, rows, :], write
    )
    for d in range(count):
        layout(early + d, rows_ref.at[d])


def last_terms(own, places, ways, done, orbs, row_blocks):
    slots = own[0].shape[0]
    nd = done.shape[0]
    count = len(ways)
    flat = [way for each in ways for way in each]
    specs = [pl.BlockSpec(memory_space=pl.ANY)] * len(flat)
    specs += [orb_spec(row_blocks, orbs, lambda r, c, p: p[0]), whole(done)]
    return call(
        functools.partial(last_kernel, count, len(ways[0])), "last_terms", [*own, places],
        [*flat, orbs, done], specs,
        jax.ShapeDtypeStruct((nd, slots, ROWS * LANES), F32),
        [
            pltpu.VMEM((count,) + ways[0][0].shape, F32),
            pltpu.VMEM((count, 8, TILE, LANES), F32),
            pltpu.VMEM((count, slots * ROWS, LANES), F32),
            pltpu.SemaphoreType.DMA((count,)),
        ],
        slots,
        mib=40,
    )


def tie(values, others=()):
    hbm = pl.BlockSpec(memory_space=pl.ANY)
    count = len(values)
    return pl.pallas_call(
        lambda *refs: None,
        out_shape=[jax.ShapeDtypeStruct(v.shape, v.dtype) for v in values],
        in_specs=[hbm] * (count + len(others)),
        out_specs=[hbm] * count,
        input_output_aliases={k: k for k in range(count)},
        name="tie",
    )(*values, *others)


def ring_order(count):
    return list(range(0, count, 2)) + list(range(count - 1, 0, -2))


def row_broadcast(value, row_count, col_count, ratio, held=None):
    def send(k):
        parent = k & (k - 1)
        if k & 1:
            rows = [[(r, r ^ 1) for r in range(row_count)]] * col_count
        else:
            rows = [[(c // ratio ^ parent, c // ratio ^ k)] for c in range(col_count)]
        pairs = [(a * col_count + c, b * col_count + c) for c in range(col_count) for a, b in rows[c]]
        return lax.ppermute(ways[parent], ("row", "col"), pairs)

    ways = [value] + [None] * (row_count - 1)
    for k in range(2, row_count, 2):
        ways[k] = send(k)
    if held is not None:
        mark = held()
        for k in range(2, row_count, 2):
            ways[k] = tie([ways[k]], [mark])[0]
    for k in range(1, row_count, 2):
        ways[k] = send(k)
    return ways


def local(
    density_tiles,
    tile_ids,
    batch_blocks,
    basis_values,
    grid_weight,
    xc_kernel,
    grid_coord,
    orbitals,
    precond_diag,
    orbital_energy,
):
    row_count = lax.axis_size("row")
    col_count = lax.axis_size("col")
    device_count = row_count * col_count
    own_row = lax.axis_index("row")
    own_col = lax.axis_index("col")
    own_index = own_row * col_count + own_col
    block_count = NB // TILE
    row_blocks = block_count // row_count
    col_blocks = block_count // col_count
    per_range = FB // row_count
    slot_count = tile_ids.shape[0]
    ratio = col_count // row_count
    col_width = col_blocks * TILE
    nd = density_tiles.shape[0]
    nocc = orbitals.shape[1]

    ask = batch_blocks
    match = ask // col_blocks == own_col
    ask_col = jnp.sum(jnp.where(match, ask, 0), axis=1)
    ask_row = lax.dynamic_slice_in_dim(ask, own_row * per_range, per_range, 1)
    wanted = jnp.where(jnp.any(match, axis=1)[:, None], ask_row * block_count + ask_col[:, None], -1)
    hit = wanted.reshape(-1)[:, None] == tile_ids[None, :]
    slots = jnp.max(jnp.where(hit, jnp.arange(slot_count, dtype=jnp.int32)[None, :], -1), axis=1)
    own_cols = lax.dynamic_slice_in_dim(ask, own_index, 1, 0)[0] // col_blocks

    local_rows = tile_ids // block_count - own_row * row_blocks
    local_cols = tile_ids % col_blocks

    order = ring_order(col_count)
    place = [order.index(c) for c in range(col_count)]
    forward = [(order[i], order[(i + 1) % col_count]) for i in range(col_count)]
    backward = [(b, a) for a, b in forward]
    ring = jnp.asarray(order, jnp.int32)
    at = jnp.asarray(place, jnp.int32)[own_col]
    part = own_col % ratio
    half = slot_count // 2
    steps = col_count // 2 - 1

    diag = precond_diag.reshape(row_blocks, ROWS, 2).swapaxes(1, 2).reshape(row_blocks, TILE, 1)
    term_place = jnp.stack([own_row, own_row ^ (own_col // ratio), own_col])

    all_orbitals = lax.all_gather(orbitals, "row", axis=0, tiled=True)
    pad = -slot_count % (8 * LANES)
    ids = jnp.pad(tile_ids, (0, pad)).reshape(-1, LANES).astype(F32)
    picked = pick_tiles(slots, density_tiles, ids, device_count)
    exchange = lambda a: lax.all_to_all(
        a, ("row", "col"), split_axis=0, concat_axis=0, tiled=True
    )
    arrived = exchange(picked)
    listed = lax.dynamic_slice(
        arrived, (own_row * col_count, arrived.shape[1] - ids.shape[0], 0), (col_count,) + ids.shape
    )
    listed = listed.reshape(col_count, -1)[:, :slot_count].astype(jnp.int32)
    listed_rows = listed // block_count - own_row * row_blocks
    listed_cols = listed % col_blocks

    def plan(offsets):
        cols = ring[(at + jnp.asarray(offsets, jnp.int32)) % col_count]
        rows = listed_rows[cols].reshape(-1)
        blocks = listed_cols[cols].reshape(-1)
        return rows, blocks, jnp.append(cols, part)

    plans = [plan((0, -1, 1))]
    plans += [plan((-step, step)) for step in range(2, steps)]
    plans[-1:] = [plan((-steps + 1, steps - 1, -steps, steps, col_count // 2))]
    tables = (diag, local_rows, local_cols, term_place)
    arrived, tables = lax.optimization_barrier((arrived, tables))
    diag, local_rows, local_cols, term_place = tables
    built = batch_tiles(
        per_range, col_count, own_cols, arrived, basis_values[0], grid_weight, xc_kernel, grid_coord
    )
    returned = exchange(built)
    hams = add_tiles(slots, returned, slot_count, nd)

    orbs, mark = split_orbitals(all_orbitals, col_count)

    own = (local_rows, local_cols)
    energy = orbital_energy[None]
    send_up = lambda a: lax.ppermute(a, "col", forward)
    send_down = lambda a: lax.ppermute(a, "col", backward)

    marks = [mark, diag, *(table for where in plans for table in where)]
    held = tie([send_up(a) for a in hams] + [send_down(a) for a in hams], marks)
    ups, downs = list(held[:2]), list(held[2:])
    totals = None
    for step in range(2, steps):
        chunks = [hams, ups, downs] if totals is None else [ups, downs]
        sums = add_rows(totals, chunks, plans[step - 2], orbs, row_blocks, col_blocks)
        up, down = send_up(ups[0]), send_down(downs[0])
        if step < steps - 1:
            ups[1], downs[1] = send_up(ups[1]), send_down(downs[1])
        ups[0], downs[0], ups[1], downs[1], *totals = tie([up, down, ups[1], downs[1], *sums])

    def opposite(up, down):
        return [send_up(up[:, :half]), send_down(down[:, half:])]

    def finish(d, chunks):
        return response_piece(
            totals[d], chunks, d % (nd - 1), plans[-1], orbs, diag, energy, col_blocks
        )

    def spread(piece, held=None):
        return row_broadcast(piece, row_count, col_count, ratio, held)

    up3, down3, *totals = tie([send_up(ups[0]), send_down(downs[0]), *totals])
    pieces, sums, ways = [], [], []
    held = tie([*opposite(up3[:1], down3[:1]), up3, down3, ups[1], downs[1], *totals])
    for d in range(nd - 1):
        up_end, down_end, up3, down3, ups[1], downs[1], *totals[d:] = held
        later = [up_end, down_end]
        if d < nd - 2:
            later = opposite(up3[d + 1 : d + 2], down3[d + 1 : d + 2])
        if d == 0:
            last2 = [send_up(ups[1]), send_down(downs[1])]
        if d == nd - 2:
            last3 = [send_up(last2[0]), send_down(last2[1])]
        piece, total = finish(d, [ups[0], downs[0], up3, down3, up_end, down_end])
        pieces.append(piece)
        sums.append(total)
        ways.append(spread(piece) if d == 0 else None)
        if d < nd - 2:
            held = tie([*later, up3, down3, *last2, *totals[d + 1 :]], [total])
            last2 = held[4:6]
    last2 = list(last2)
    last3[0], last3[1], last2[0], last2[1], totals[-1] = tie([*last3, *last2, totals[-1]], [sums[-1]])
    up_end, down_end, *last3, last2[0], last2[1], totals[-1] = tie(
        [*opposite(*last3), *last3, *last2, totals[-1]], [ways[0][row_count // 2]]
    )
    piece, total = finish(nd - 1, [*last2, *last3, up_end, down_end])
    sums.append(total)
    ways = ways[:1]
    piece = tie([piece], [ways[0][row_count // 2]])[0]
    done = early_terms(own, term_place, ways, sums, diag, energy, orbs, row_blocks, col_blocks)
    for value in [*pieces[1:], piece]:
        ways.append(spread(value, lambda: done))
    return last_terms(own, term_place, ways[1:], done, orbs, row_blocks)


def solution(mesh):
    placed = (
        P(None, ("row", "col"), None),
        P(("row", "col")),
        P(),
        P(("row", "col"), None, None),
        P(("row", "col"), None),
        P(("row", "col"), None),
        P(None, ("row", "col"), None),
        P("row", None),
        P("row"),
        P(),
    )
    return jax.shard_map(
        local, mesh=mesh, in_specs=placed, out_specs=P(None, ("row", "col"), None), check_vma=False
    )
```
